256 devices in a mesh: gx: 16 (over z_hi, y), gy: 16 (over z_lo, x, core).
Axes of the slice: x: 4, y: 4, z: 8 (z_hi: 4, z_lo: 2; z = z_hi * 2 + z_lo), core: 2. Of those that a mesh axis runs over, the one named last changes fastest.
Arguments:
- face_trans: float32 [3, 256, 256, 128], P(None, 'gx', 'gy'), may hold values from 0.002 to 0.2
- partition: int32 [256, 256, 128], P('gx', 'gy'), may hold values from 0 to 26, as said below
- support_pad: int32 [6, 32, 32, 16], P(None, 'gx', 'gy'), may hold values from 1 to 3
- owners: int32 [16, 16, 64, 1], P('gx', 'gy'), may hold values from 0 to 15; in each aligned block of 64 rows (0 to 63, 64 to 127, ..., all dimensions but the last counted through in order) at most 8 rows name the same one
Outputs:
- prolongation: float32 [8, 256, 256, 128], P(None, 'gx', 'gy')
- coarse_rows: float32 [16, 16, 27, 128], P('gx', 'gy')
The draws below stay inside these ranges and needn't reach their ends.
Inputs may be any that keep to these rules, and one draw needn't show every extreme that they name: `partition`: each cell's own block is the block holding a position that lies in the grid and differs from the cell by at most one cell in each dimension. `owners`: among the blocks of one device, no owner index is named more than 8 times, a bound that some block reaches.
All inputs are finite; a program needn't handle non-finite values.
Results may differ from the reference program's by a relative error of at most 0.0001.
Values sent between devices are 32-bit elements; how exact they have to be, the bound alone decides.
A program may use at most 128 MiB of HBM per device.

```python
import math
import jax
import jax.numpy as jnp
import numpy as np
from jax import lax

B = 8
H = 4
ITERS = 2
NBXD = 2
NBYD = 2
NBZ = 16
NB_DEV = 64
NX = 256
NY = 256
NZ = 128
NBX = 32
NBY = 32
CAP = 8
N_GX = 16
N_GY = 16


def draw_partition(key, part):
    subkeys = jax.random.split(key, 3)
    shape = (NX, NY, NZ)
    grid_x = jnp.arange(NX, dtype=jnp.int32)[:, None, None]
    grid_y = jnp.arange(NY, dtype=jnp.int32)[None, :, None]
    grid_z = jnp.arange(NZ, dtype=jnp.int32)[None, None, :]
    moved_x = jnp.clip(grid_x + jax.random.randint(subkeys[0], shape, -1, 2, dtype=jnp.int32), 0, NX - 1) // B
    moved_y = jnp.clip(grid_y + jax.random.randint(subkeys[1], shape, -1, 2, dtype=jnp.int32), 0, NY - 1) // B
    moved_z = jnp.clip(grid_z + jax.random.randint(subkeys[2], shape, -1, 2, dtype=jnp.int32), 0, NZ - 1) // B
    step_x = moved_x - grid_x // B + 1
    step_y = moved_y - grid_y // B + 1
    step_z = moved_z - grid_z // B + 1
    return (step_x * 9 + step_y * 3 + step_z).astype(jnp.int32)


def set_ends(result, own_key, low, high):
    extent = result.shape
    index_at = [jax.random.randint(jax.random.fold_in(own_key, axis), (), 0, extent[axis]) for axis in range(len(extent))]
    result = result.at[tuple(index_at)].set(low)
    longest = extent.index(max(extent))
    index_at[longest] = (index_at[longest] + 1) % extent[longest]
    return result.at[tuple(index_at)].set(high)


def block_scale(key, dims, shards, low, top_value):
    def one(dim, parts):
        draws = jax.random.uniform(jax.random.fold_in(jax.random.fold_in(key, 6), dim), (parts,), jnp.float32, low / len(shards), top_value / len(shards))
        return jnp.repeat(jnp.exp(draws), dims[dim] // parts).reshape((-1,) + (1,) * (len(dims) - dim - 1))

    level = one(*shards[0])
    for cut in shards[1:]:
        level = level * one(*cut)
    return level


def deal_out(rng, own, number, rows, number_of, top, reach, skew):
    ranking = jax.random.permutation(rng, number_of)
    heavy_load, common = shares(number_of, rows * top, reach, skew, True), shares(number_of, rows * top, reach, skew, False)
    places = jnp.arange(number_of)

    def named(tallies, turn):
        used = int((tallies > 0).sum())
        fixed = max(1, used // 4)
        passed = fixed + (places - fixed + turn * (used - fixed)) % max(1, number_of - fixed)
        return jnp.zeros((number_of,), jnp.int32).at[ranking[jnp.where(places < fixed, places, passed)]].set(jnp.asarray(tallies, jnp.int32))

    tallies = jnp.where(number % 4 == 0, named(heavy_load, number // 4), named(common, number - number // 4 - 1))
    mixed = jax.random.permutation(jax.random.fold_in(own, 3), number_of)
    donor, taker = mixed[0:number_of // 2 * 2:2], mixed[1:number_of // 2 * 2:2]
    slack = jnp.minimum(tallies[donor] - 1, reach - tallies[taker]) // 2
    slack = jnp.where((donor == ranking[0]) | (taker == ranking[0]) | (tallies[taker] == 0), 0, jnp.maximum(slack, 0))
    passed = jax.random.randint(jax.random.fold_in(own, 4), (number_of // 2,), 0, 1 << 20) % (slack + 1)
    tallies = tallies.at[donor].add(-passed).at[taker].add(passed)
    items = jnp.searchsorted(jnp.cumsum(tallies), jnp.arange(rows * top), side="right").astype(jnp.int32)
    listing = items.reshape(top, rows).T
    listing = listing[jax.random.permutation(jax.random.fold_in(own, 1), rows)]
    turn = jax.random.randint(jax.random.fold_in(own, 2), (rows, 1), 0, top)
    return jnp.take_along_axis(listing, (jnp.arange(top)[None, :] + turn) % top, axis=1)


def shares(count, total, reach, skew, full):
    loads = [(1 << 20) // math.isqrt(grade ** skew) + 1 for grade in range(1, count + 1)]
    largest = reach if full else min(reach, max(-(-total // count), total * loads[0] // sum(loads)))
    least = 1 if total - largest >= count - 1 else 0
    given, spare = [largest] + [least] * (count - 1), total - largest - least * (count - 1)
    while spare > 0:
        free = [i for i in range(1, count) if given[i] < largest] or [i for i in range(1, count) if given[i] < reach]
        mass, budget = sum([loads[i] for i in free]), spare
        for i in free:
            addition = min(reach - given[i], max(1, budget * loads[i] // mass), spare)
            given[i] = given[i] + addition
            spare = spare - addition
    return np.array(given)


def setup_inputs(seed: int = 0) -> dict:
    arg_keys = jax.random.split(jax.random.key(seed), 5)
    face_trans = jnp.clip(jnp.exp(math.log(0.2) - 4.6051702 * jax.random.uniform(arg_keys[0], (3, NX, NY, NZ), jnp.float32) ** block_scale(arg_keys[0], (3, NX, NY, NZ), ((1, 16), (2, 16)), -0.2, 0.2)), 0.002, 0.2)
    partition = draw_partition(jax.random.fold_in(arg_keys[4], 71), 0)
    support_pad = set_ends(jax.random.randint(arg_keys[2], (6, NBX, NBY, NBZ), 1, H), jax.random.fold_in(arg_keys[2], 1), 1, H - 1).astype(jnp.int32)
    owners_keys = jax.random.split(jax.random.fold_in(arg_keys[3], 1), N_GX * N_GY * NB_DEV // NB_DEV)
    owners_turns = jax.random.permutation(jax.random.fold_in(arg_keys[3], 3), N_GX * N_GY * NB_DEV // NB_DEV)
    owners = jax.vmap(lambda own, number: deal_out(jax.random.fold_in(arg_keys[3], 2), own, number, NB_DEV, N_GY, 1, CAP, 2))(owners_keys, owners_turns).reshape((N_GX, N_GY, NB_DEV, 1))
    return dict(face_trans=face_trans, partition=partition, support_pad=support_pad, owners=owners)


relax = 2.0 / 3.0
highest = lax.Precision.HIGHEST


def slot_cover(position, parity):
    blocks = position // B
    toward = jnp.where(position % B >= H, 1, -1)
    cover_block = jnp.where(blocks % 2 == parity, blocks, blocks + toward)
    offset = (position + H + parity * B) % (2 * B)
    return cover_block, offset


def stencil(padded, faces, diagonal):
    west_trans, east_trans, south_trans, north_trans, bottom_trans, top_trans = faces
    centre = padded[..., 1:-1, 1:-1, :]
    zero_layer = jnp.zeros_like(centre[..., :1])
    above = jnp.concatenate([centre[..., 1:], zero_layer], -1)
    below = jnp.concatenate([zero_layer, centre[..., :-1]], -1)
    return (diagonal * centre - east_trans * padded[..., 2:, 1:-1, :] - west_trans * padded[..., :-2, 1:-1, :]
            - north_trans * padded[..., 1:-1, 2:, :] - south_trans * padded[..., 1:-1, :-2, :]
            - top_trans * above - bottom_trans * below)


def coarse_table(halves, margin, span):
    half_index = jnp.arange(halves, dtype=jnp.int32)
    blocks = half_index // 2
    toward = jnp.where(half_index % 2 == 1, 1, -1)
    bit_values = jnp.arange(2, dtype=jnp.int32)
    cover_block = jnp.where(blocks[None, :] % 2 == bit_values[:, None], blocks[None, :], blocks[None, :] + toward[None, :])
    target = blocks[None, :] + bit_values[:, None] * toward[None, :]
    places = jnp.arange(span, dtype=jnp.int32)
    codes = jnp.arange(3, dtype=jnp.int32)
    hit_target = target[:, :, None] + margin == places[None, None, :]
    hit_code = cover_block[:, None, :, None] - target[None, :, :, None] + 1 == codes[None, None, None, :]
    return (hit_target[None, :, :, :, None] & hit_code[:, :, :, None, :]).astype(jnp.float32)


def reference(face_trans, partition, support_pad, owners):
    along_x = jnp.arange(NX, dtype=jnp.int32)
    along_y = jnp.arange(NY, dtype=jnp.int32)
    along_z = jnp.arange(NZ, dtype=jnp.int32)
    east_trans = face_trans[0] * (along_x < NX - 1)[:, None, None]
    north_trans = face_trans[1] * (along_y < NY - 1)[None, :, None]
    top_trans = face_trans[2] * (along_z < NZ - 1)[None, None, :]
    west_trans = jnp.pad(east_trans[:-1], ((1, 0), (0, 0), (0, 0)))
    south_trans = jnp.pad(north_trans[:, :-1], ((0, 0), (1, 0), (0, 0)))
    bottom_trans = jnp.pad(top_trans[:, :, :-1], ((0, 0), (0, 0), (1, 0)))
    faces = (west_trans, east_trans, south_trans, north_trans, bottom_trans, top_trans)
    diagonal = west_trans + east_trans + south_trans + north_trans + bottom_trans + top_trans
    block_x = (along_x // B)[:, None, None]
    block_y = (along_y // B)[None, :, None]
    block_z = (along_z // B)[None, None, :]
    part_x = block_x + partition // 9 - 1
    part_y = block_y + (partition // 3) % 3 - 1
    part_z = block_z + partition % 3 - 1
    pad_cycle = jnp.pad(support_pad, ((0, 0), (1, 1), (1, 1), (1, 1)))
    supports = []
    starts = []
    for slot_id in range(8):
        cover_x, offset_x = slot_cover(along_x, (slot_id >> 2) & 1)
        cover_y, offset_y = slot_cover(along_y, (slot_id >> 1) & 1)
        cover_z, offset_z = slot_cover(along_z, slot_id & 1)
        inside = None
        offsets = (offset_x[:, None, None], offset_y[None, :, None], offset_z[None, None, :])
        for dim_id in range(3):
            table = pad_cycle[2 * dim_id:2 * dim_id + 2]
            table = jnp.take(table, cover_x + 1, axis=1)
            table = jnp.take(table, cover_y + 1, axis=2)
            table = jnp.take(table, cover_z + 1, axis=3)
            along_ok = (offsets[dim_id] + table[0] >= H) & (offsets[dim_id] <= H + B - 1 + table[1])
            inside = along_ok if inside is None else inside & along_ok
        supports.append(inside)
        starts.append((cover_x[:, None, None] == part_x) & (cover_y[None, :, None] == part_y)
                      & (cover_z[None, None, :] == part_z))
    basis_slots = jnp.stack(starts).astype(jnp.float32)
    for step_id in range(ITERS):
        updated = []
        for slot_id in range(8):
            applied = stencil(jnp.pad(basis_slots[slot_id], ((1, 1), (1, 1), (0, 0))), faces, diagonal)
            updated.append(supports[slot_id] * (basis_slots[slot_id] - relax * applied / diagonal))
        updated = jnp.stack(updated)
        basis_slots = updated / jnp.sum(updated, 0)
    move_code = ((part_x != block_x).astype(jnp.int32) * 4 + (part_y != block_y).astype(jnp.int32) * 2
                 + (part_z != block_z).astype(jnp.int32))
    half_count = (NX // H) * (NY // H) * (NZ // H)
    half_index = (((along_x // H)[:, None, None] * (NY // H) + (along_y // H)[None, :, None]) * (NZ // H)
                  + (along_z // H)[None, None, :])
    segment_ids = (move_code * half_count + half_index).reshape(-1)
    cube_list = []
    for slot_id in range(8):
        applied = stencil(jnp.pad(basis_slots[slot_id], ((1, 1), (1, 1), (0, 0))), faces, diagonal)
        cube_list.append(jax.ops.segment_sum(applied.reshape(-1), segment_ids, num_segments=8 * half_count))
    cube_sums = jnp.stack(cube_list).reshape(2, 2, 2, 2, 2, 2, NX // H, NY // H, NZ // H)
    table_x = coarse_table(NX // H, 0, NBX)
    table_y = coarse_table(NY // H, 0, NBY)
    table_z = coarse_table(NZ // H, 0, NBZ)
    acc = jnp.einsum("abcdefxyz,adxio->bcefyzio", cube_sums, table_x, precision=highest)
    acc = jnp.einsum("bcefyzio,beyjp->cfzijop", acc, table_y, precision=highest)
    acc = jnp.einsum("cfzijop,cfzkr->oprijk", acc, table_z, precision=highest)
    coarse = acc.reshape(27, NBX, NBY, NBZ)
    per_device = coarse.reshape(27, N_GX, NBXD, N_GY, NBYD, NBZ).transpose(1, 3, 0, 2, 4, 5)
    per_device = per_device.reshape(N_GX, N_GY, 27, NB_DEV)
    owner_ids = owners[..., 0]
    matches = (owner_ids[..., None] == jnp.arange(N_GY, dtype=jnp.int32)).astype(jnp.int32)
    ranks = jnp.cumsum(matches, axis=2) - matches
    placing = (matches[..., None] * (ranks[..., None] == jnp.arange(CAP, dtype=jnp.int32))).astype(jnp.float32)
    routed = jnp.einsum("gskl,gslor->goksr", per_device, placing, precision=highest)
    return basis_slots, routed.reshape(N_GX, N_GY, 27, N_GY * CAP)
```

```python
import functools

import jax
import jax.numpy as jnp
from jax import lax
from jax.experimental import pallas as pl
from jax.experimental.pallas import tpu as pltpu
from jax.sharding import PartitionSpec as P

MESH = pl.DeviceIdType.MESH
F32 = jnp.float32
HIGHEST = lax.Precision.HIGHEST

E = 24
FY, FZ, FX, CODE = range(4)
AROUND = [(dx, dy) for dx in (-1, 0, 1) for dy in (-1, 0, 1) if (dx, dy) != (0, 0)]
SUM_START = (-1, 4, 7, 12)
SUM_MASKED = ((0, 1), (3, 4), (0, 1), (3, 4))


def iota(shape, dim):
    return lax.broadcasted_iota(jnp.int32, shape, dim)


def dot(a, b):
    return lax.dot_general(a, b, (((1,), (0,)), ((), ())), precision=HIGHEST, preferred_element_type=F32)


def dot_nt(a, b):
    return lax.dot_general(a, b, (((1,), (1,)), ((), ())), precision=HIGHEST, preferred_element_type=F32)


def kernel(n_x, n_y, ft, pt, sp, ow, pro, rows_out,
           own, rxl, rxh, ypl, yph, ryl, ryh, pd, rp, pe, ex, yz, fe, cf, mk, ba, bb, ap, wm, acc, xs, ct, pp, orow,
           snd, rcv, x_send, x_recv, y_send, y_recv, p_send, p_recv, e_send, e_recv):
    gx = lax.axis_index("gx")
    gy = lax.axis_index("gy")
    peer = lambda dx, dy: (lax.rem(gx + (dx + n_x), n_x), lax.rem(gy + (dy + n_y), n_y))

    barrier = pltpu.get_barrier_semaphore()
    far = [j for j in range(1, n_y) if j not in (1, n_y - 1)]
    for dx, dy in AROUND:
        pl.semaphore_signal(barrier, inc=1, device_id=peer(dx, dy), device_id_type=MESH)
    for j in far:
        pl.semaphore_signal(barrier, inc=1, device_id=peer(0, j), device_id_type=MESH)

    pd[...] = jnp.zeros((8, 128), F32)
    for bx in range(2):
        total = None
        for k in range(6):
            place = (iota((16, 128), 1) == iota((16, 128), 0) + 16 * k).astype(F32)
            term = dot(sp[k, bx].astype(F32), place)
            total = term if total is None else total + term
        pd[2 * bx:2 * bx + 2, :] = total

    x_last = gx == n_x - 1
    y_last = gy == n_y - 1
    row16 = iota((16, 128), 0)
    lane16 = iota((16, 128), 1)
    keep_y = jnp.where((row16 == 15) & y_last, 0.0, 1.0)
    keep_z = jnp.where(lane16 == 127, 0.0, 1.0)

    def stage(x, carry):
        keep_x = jnp.where((x == 15) & x_last, 0.0, 1.0)
        p = pt[x]
        px = (p >= 9).astype(jnp.int32) + (p >= 18).astype(jnp.int32)
        q = p - 9 * px
        py = (q >= 3).astype(jnp.int32) + (q >= 6).astype(jnp.int32)
        pz = q - 3 * py
        bx = ((x >> 3) + px + 1) & 1
        by = ((row16 >> 3) + py + 1) & 1
        bz = ((lane16 >> 3) + pz + 1) & 1
        code = (4 * bx + 2 * by + bz).astype(F32)
        values = {FX: ft[0, x] * keep_x, FY: ft[1, x] * keep_y, FZ: ft[2, x] * keep_z, CODE: code}
        for k in range(4):
            own[x * 4 + k] = values[k]
            fe[k, x + 4, 12:28, :] = values[k]
            start = pl.multiple_of(x * 16, 8) + 4 * k
            ypl[pl.ds(start, 4), :] = values[k][0:4]
            yph[pl.ds(start, 4), :] = values[k][12:16]
        return carry

    lax.fori_loop(0, 16, stage, 0)
    pl.semaphore_wait(barrier, 8 + len(far))

    def remote(src, dst, send, recv, dx, dy):
        copy = pltpu.make_async_remote_copy(src_ref=src, dst_ref=dst, send_sem=send, recv_sem=recv,
                                            device_id=peer(dx, dy), device_id_type=MESH)
        copy.start()
        return copy

    pad_copies = [
        remote(pd, rp.at[pl.ds(8 * d, 8)], p_send.at[d], p_recv.at[d], dx, dy) for d, (dx, dy) in enumerate(AROUND)
    ]
    halo = [
        remote(own.at[pl.ds(50, 14)], rxl, x_send.at[0], x_recv.at[0], 1, 0),
        remote(own.at[pl.ds(0, 12)], rxh.at[pl.ds(0, 12)], x_send.at[1], x_recv.at[1], -1, 0),
        remote(own.at[pl.ds(15, 1)], rxh.at[pl.ds(12, 1)], x_send.at[2], x_recv.at[2], -1, 0),
        remote(yph, ryl.at[pl.ds(64, 256)], y_send.at[0], y_recv.at[0], 0, 1),
        remote(ypl, ryh.at[pl.ds(64, 256)], y_send.at[1], y_recv.at[1], 0, -1),
        remote(yph.at[pl.ds(192, 64)], ryl.at[pl.ds(0, 64)], y_send.at[2], y_recv.at[2], 1, 1),
        remote(yph.at[pl.ds(0, 64)], ryl.at[pl.ds(320, 64)], y_send.at[3], y_recv.at[3], -1, 1),
        remote(ypl.at[pl.ds(192, 64)], ryh.at[pl.ds(0, 64)], y_send.at[4], y_recv.at[4], 1, -1),
        remote(ypl.at[pl.ds(0, 64)], ryh.at[pl.ds(320, 64)], y_send.at[5], y_recv.at[5], -1, -1),
    ]

    zero8 = jnp.zeros((8, 128), F32)

    def clear(x, carry):
        for s in range(8):
            for b in (ba, bb):
                b[s, x, 0:8, :] = zero8
                b[s, x, 32:40, :] = zero8
        for k in range(4):
            fe[k, x, 0:8, :] = zero8
        return carry

    lax.fori_loop(0, E, clear, 0)

    orow[...] = jnp.full((8, 128), -1.0, F32)
    orow[0:1, 0:64] = ow[...].astype(F32)
    owner = jnp.broadcast_to(orow[0:1, :], (128, 128))
    earlier = (owner == owner.T) & (iota((128, 128), 0) < iota((128, 128), 1))
    rank = jnp.sum(earlier.astype(F32), axis=0, keepdims=True)
    target = orow[0:1, :] * 8.0 + rank
    row_f = iota((128, 128), 0).astype(F32)
    for b in range(4):
        shifted = jnp.broadcast_to(target, (8, 128))
        if b:
            shifted = pltpu.roll(shifted, 128 - 16 * b, 1)
        pp[b] = ((row_f == shifted[0:1]) & (iota((128, 128), 1) < 16)).astype(F32)

    c = iota((128, 256), 1)
    up_z, b_x, up_x, b_y, up_y = c >> 7, (c >> 6) & 1, (c >> 5) & 1, (c >> 4) & 1, (c >> 3) & 1
    s_x, s_y, s_z = (c >> 2) & 1, (c >> 1) & 1, c & 1
    o_x = jnp.where(s_x == b_x, 1, 2 * up_x)
    o_y = jnp.where(s_y == b_y, 1, 2 * up_y)
    o_z = jnp.where(s_z == 0, 1, 2 * up_z)
    ct[...] = (iota((128, 256), 0) == (b_x * 2 + b_y) * 32 + 9 * o_x + 3 * o_y + o_z).astype(F32)

    for copy in pad_copies:
        copy.wait_recv()
    low = {-1: 0, 0: 1, 1: 3}
    for dx, dy in AROUND + [(0, 0)]:
        sx, sy = -dx, -dy
        base = 0 if (dx, dy) == (0, 0) else 8 * AROUND.index((dx, dy))
        src = pd if (dx, dy) == (0, 0) else rp
        for i in ((1,) if sx < 0 else (0,) if sx > 0 else (0, 1)):
            for j in ((1,) if sy < 0 else (0,) if sy > 0 else (0, 1)):
                bi = low[sx] + (i if sx == 0 else 0)
                bj = low[sy] + (j if sy == 0 else 0)
                pe[4 * bi + bj:4 * bi + bj + 1, :] = src[base + 2 * i + j:base + 2 * i + j + 1, :]
    block_row = iota((16, 128), 0)
    outside = ((((block_row >> 2) == 0) & (gx == 0)) | (((block_row >> 2) == 3) & x_last)
               | (((block_row & 3) == 0) & (gy == 0)) | (((block_row & 3) == 3) & y_last))
    pads = jnp.where(outside, 0.0, pe[...])
    r_in = iota((128, 128), 0)
    tile_z = (iota((128, 128), 1) + 4) >> 3
    for sz in range(2):
        upper = (tile_z & 1) == sz
        bz = jnp.where(upper, tile_z, tile_z - 1)
        fits = (bz >= 0) & (bz < 16)
        for k in range(5):
            lanes = bz + 16 * k if k < 4 else bz + jnp.where(upper, 64, 80)
            ex[sz * 5 + k] = dot(pads, (fits & (r_in == lanes)).astype(F32))

    row8 = iota((8, 128), 0).astype(F32)
    lane8 = iota((8, 128), 1)
    i_z = ((lane8 + 4) & 7).astype(F32)
    up8 = ((lane8 + 4) >> 3) & 1
    for s in range(8):
        sx, sy, sz = s >> 2, (s >> 1) & 1, s & 1
        for g in range(3):
            bx = g if g % 2 == sx else g - 1
            for t in range(3):
                by = t if t % 2 == sy else t - 1
                r = (bx + 1) * 4 + by + 1
                reach_z = ex[sz * 5 + 4, r:r + 1, :]
                ok_z = jnp.where(up8 == sz, i_z + reach_z, 7.0 - i_z + reach_z) >= 4.0
                if by == t:
                    ok_y = row8 + ex[sz * 5 + 2, r:r + 1, :] >= 4.0
                else:
                    ok_y = row8 <= 3.0 + ex[sz * 5 + 3, r:r + 1, :]
                yz[s, g, 8 * t:8 * t + 8, :] = (ok_z & ok_y).astype(F32)

    def masks(i, carry):
        at = i.astype(F32)
        for s in range(8):
            sx, sy, sz = s >> 2, (s >> 1) & 1, s & 1
            for g in range(3):
                bx = g if g % 2 == sx else g - 1
                for t in range(3):
                    by = t if t % 2 == sy else t - 1
                    r = (bx + 1) * 4 + by + 1
                    if bx == g:
                        ok_x = ex[sz * 5, r:r + 1, :] >= 4.0 - at
                    else:
                        ok_x = ex[sz * 5 + 1, r:r + 1, :] >= at - 3.0
                    mk[s, 8 * g + i, 8 * t:8 * t + 8, :] = jnp.where(ok_x, yz[s, g, 8 * t:8 * t + 8, :], 0.0)
        return carry

    lax.fori_loop(0, 8, masks, 0)

    for copy in halo:
        copy.wait_recv()

    for i in range(14):
        flat = 50 + i
        fe[flat % 4, flat // 4 - 12, 12:28, :] = rxl[i]
    for i in range(12):
        fe[i % 4, 20 + i // 4, 12:28, :] = rxh[i]
    fe[CODE, 23, 12:28, :] = rxh[12]

    def unpack(x, carry):
        for k in range(4):
            start = pl.multiple_of(x * 16, 8) + 4 * k
            fe[k, x, 8:12, :] = ryl[pl.ds(start, 4), :]
            fe[k, x, 28:32, :] = ryh[pl.ds(start, 4), :]
        return carry

    lax.fori_loop(0, E, unpack, 0)

    def first(x, carry):
        for t in range(3):
            code = fe[CODE, x, 8 + 8 * t:16 + 8 * t, :]
            for s in range(8):
                ba[s, x, 8 + 8 * t:16 + 8 * t, :] = (code == float(s)).astype(F32)
        return carry

    lax.fori_loop(0, E, first, 0)

    def coefficients(x, carry):
        for t in range(3):
            a, b = 8 + 8 * t, 16 + 8 * t
            east, west = fe[FX, x, a:b, :], fe[FX, x - 1, a:b, :]
            north, south = fe[FY, x, a:b, :], fe[FY, x, a - 1:b - 1, :]
            top = fe[FZ, x, a:b, :]
            bottom = pltpu.roll(top, 1, 1)
            diagonal = west + east + south + north + bottom + top
            inverse = 1.0 / diagonal
            for i, face in enumerate((east, west, north, south, top, bottom)):
                cf[i, x, 8 * t:8 * t + 8, :] = face * inverse
            cf[6, x, 8 * t:8 * t + 8, :] = diagonal
        return carry

    lax.fori_loop(1, E - 1, coefficients, 0)

    def around(src, s, x, t, faces):
        east, west, north, south, top, bottom = faces
        a, b = 8 + 8 * t, 16 + 8 * t
        centre = src[s, x, a:b, :]
        total = (east * src[s, x + 1, a:b, :] + west * src[s, x - 1, a:b, :]
                 + north * src[s, x, a + 1:b + 1, :] + south * src[s, x, a - 1:b - 1, :]
                 + top * pltpu.roll(centre, 127, 1) + bottom * pltpu.roll(centre, 1, 1))
        return centre, total

    def smooth(src, dst, x, carry):
        for t in range(3):
            faces = [cf[i, x, 8 * t:8 * t + 8, :] for i in range(6)]
            updated = []
            for s in range(8):
                centre, total = around(src, s, x, t, faces)
                updated.append(mk[s, x, 8 * t:8 * t + 8, :] * (0.5 * centre + total))
            whole = ((updated[0] + updated[1]) + (updated[2] + updated[3])) + (
                (updated[4] + updated[5]) + (updated[6] + updated[7]))
            scale = 1.0 / jnp.where(whole > 0.0, whole, 1.0)
            for s in range(8):
                dst[s, x, 8 + 8 * t:16 + 8 * t, :] = updated[s] * scale
        return carry

    lax.fori_loop(1, E - 1, functools.partial(smooth, ba, bb), 0)
    lax.fori_loop(2, E - 2, functools.partial(smooth, bb, ba), 0)

    def give(x, carry):
        for s in range(8):
            pro[s, x] = ba[s, x + 4, 12:28, :]
        return carry

    lax.fori_loop(0, 16, give, 0)

    def apply(x, carry):
        for t in range(3):
            faces = [cf[i, x, 8 * t:8 * t + 8, :] for i in range(6)]
            diagonal = cf[6, x, 8 * t:8 * t + 8, :]
            for s in range(8):
                centre, total = around(ba, s, x, t, faces)
                ap[s, x, 8 * t:8 * t + 8, :] = diagonal * (centre - total)
        return carry

    lax.fori_loop(3, E - 3, apply, 0)

    for a in range(4):
        for i in range(5):
            x = SUM_START[a] + 4 + i
            for t in range(3):
                code = fe[CODE, x, 8 + 8 * t:16 + 8 * t, :].astype(jnp.int32)
                in_x = (((code >> 2) & 1) == a // 2).astype(F32)
                odd_y = ((code >> 1) & 1).astype(F32)
                odd_z = (code & 1).astype(F32)
                in_y = 1.0 - odd_y if t == 0 else odd_y
                wm[a * 5 + i, 0, 8 * t:8 * t + 8, :] = in_x
                wm[a * 5 + i, 1, 8 * t:8 * t + 8, :] = in_x * odd_z
                wm[a * 5 + i, 2, 8 * t:8 * t + 8, :] = in_x * in_y
                wm[a * 5 + i, 3, 8 * t:8 * t + 8, :] = in_x * in_y * odd_z

    def sums(s, carry):
        for a in range(4):
            for t in range(3):
                parts = [None] * 4
                for i in range(5):
                    value = ap[s, SUM_START[a] + 4 + i, 8 * t:8 * t + 8, :]
                    for m in range(4) if t == 1 else (2, 3):
                        if m == 0 and i not in SUM_MASKED[a]:
                            term = value
                        else:
                            term = value * wm[a * 5 + i, m, 8 * t:8 * t + 8, :]
                        parts[m] = term if parts[m] is None else parts[m] + term
                for m in range(4) if t == 1 else (2, 3):
                    place = a * 8 + (m - 2 if t == 0 else m + 2 if t == 1 else m + 4)
                    acc[pl.ds(pl.multiple_of((place * 8 + s) * 8, 8), 8), :] = parts[m]
        return carry

    lax.fori_loop(0, 8, sums, 0)

    def over_rows(place):
        total = acc[pl.ds(place * 64, 8, stride=8), :]
        for y in range(1, 8):
            total = total + acc[pl.ds(place * 64 + y, 8, stride=8), :]
        return total

    for a in range(4):
        r = [over_rows(a * 8 + m) for m in range(8)]
        r[2], r[3] = r[2] - r[4], r[3] - r[5]
        for b in range(4):
            for m in range(2):
                start = m * 128 + (a * 4 + b) * 8
                xs[start:start + 8, :] = r[2 * b + m]

    lane_tile = (iota((128, 128), 0) + 4) >> 3
    col = iota((128, 128), 1)
    even = (col & 1) == 0
    even_row = (iota((128, 128), 0) & 1) == 0
    halves = []
    for up in range(2):
        gather = ((lane_tile == col + up) & (col < 16)).astype(F32)
        z = dot(xs[...], gather)
        v = jnp.where(even, z[0:128] - z[128:256], z[128:256])
        other = jnp.where(even_row, pltpu.roll(v, 127, 0), pltpu.roll(v, 1, 0))
        halves.append(jnp.where(even, v, other))
    entries = dot(ct[:, 0:128], halves[0]) + dot(ct[:, 128:256], halves[1])
    routed = dot_nt(pp[0], entries[0:32])
    for b in range(1, 4):
        routed = routed + dot_nt(pp[b], entries[32 * b:32 * b + 32])
    snd[:, 0:32] = routed
    snd[:, 32:128] = jnp.zeros((128, 96), F32)

    mine = pl.multiple_of(gy * 8, 8)
    sent = []
    for j in range(1, n_y):
        there = lax.rem(gy + j, n_y)
        sent.append(remote(snd.at[pl.ds(pl.multiple_of(there * 8, 8), 8)], rcv.at[pl.ds(mine, 8)],
                           e_send.at[j], e_recv.at[j], 0, j))
    rcv[pl.ds(mine, 8), :] = snd[pl.ds(mine, 8), :]
    for copy in sent:
        copy.wait_recv()
    rows_out[...] = rcv[...].T[0:27, :]
    for copy in pad_copies + halo + sent:
        copy.wait_send()


def solution(mesh):
    n_x, n_y = mesh.shape["gx"], mesh.shape["gy"]
    vmem = pl.BlockSpec(memory_space=pltpu.VMEM)
    dma = pltpu.SemaphoreType.DMA

    def on_device(face_trans, partition, support_pad, owners):
        prolongation, rows = pl.pallas_call(
            functools.partial(kernel, n_x, n_y),
            out_shape=(
                jax.ShapeDtypeStruct((8, 16, 16, 128), F32),
                jax.ShapeDtypeStruct((27, 128), F32),
            ),
            in_specs=[vmem] * 4,
            out_specs=(vmem, vmem),
            scratch_shapes=[
                pltpu.VMEM((64, 16, 128), F32),
                pltpu.VMEM((14, 16, 128), F32),
                pltpu.VMEM((13, 16, 128), F32),
                pltpu.VMEM((256, 128), F32),
                pltpu.VMEM((256, 128), F32),
                pltpu.VMEM((384, 128), F32),
                pltpu.VMEM((384, 128), F32),
                pltpu.VMEM((8, 128), F32),
                pltpu.VMEM((64, 128), F32),
                pltpu.VMEM((16, 128), F32),
                pltpu.VMEM((10, 16, 128), F32),
                pltpu.VMEM((8, 3, E, 128), F32),
                pltpu.VMEM((4, E, 40, 128), F32),
                pltpu.VMEM((7, E, E, 128), F32),
                pltpu.VMEM((8, E, E, 128), F32),
                pltpu.VMEM((8, E, 40, 128), F32),
                pltpu.VMEM((8, E, 40, 128), F32),
                pltpu.VMEM((8, E, E, 128), F32),
                pltpu.VMEM((20, 4, E, 128), F32),
                pltpu.VMEM((2048, 128), F32),
                pltpu.VMEM((256, 128), F32),
                pltpu.VMEM((128, 256), F32),
                pltpu.VMEM((4, 128, 128), F32),
                pltpu.VMEM((8, 128), F32),
                pltpu.VMEM((128, 128), F32),
                pltpu.VMEM((8 * n_y, 128), F32),
                dma((3,)), dma((3,)), dma((6,)), dma((6,)), dma((8,)), dma((8,)), dma((n_y,)), dma((n_y,)),
            ],
            compiler_params=pltpu.CompilerParams(
                collective_id=0, has_side_effects=True, vmem_limit_bytes=48 * 2**20
            ),
        )(face_trans, partition, support_pad, owners.reshape(1, 64))
        return prolongation, rows.reshape(1, 1, 27, 128)

    placed = (
        P(None, "gx", "gy", None),
        P("gx", "gy", None),
        P(None, "gx", "gy", None),
        P("gx", "gy", None, None),
    )
    return jax.shard_map(
        on_device,
        mesh=mesh,
        in_specs=placed,
        out_specs=(P(None, "gx", "gy", None), P("gx", "gy", None, None)),
        check_vma=False,
    )
```

```python
import functools

import jax
import jax.numpy as jnp
from jax import lax
from jax.experimental import pallas as pl
from jax.experimental.pallas import tpu as pltpu
from jax.sharding import PartitionSpec as P

MESH = pl.DeviceIdType.MESH
F32 = jnp.float32
HIGHEST = lax.Precision.HIGHEST

E = 24
FY, FZ, FX, CODE = range(4)
AROUND = [(dx, dy) for dx in (-1, 0, 1) for dy in (-1, 0, 1) if (dx, dy) != (0, 0)]
SUM_START = (-1, 4, 7, 12)
SUM_MASKED = ((0, 1), (3, 4), (0, 1), (3, 4))


def iota(shape, dim):
    return lax.broadcasted_iota(jnp.int32, shape, dim)


def dot(a, b):
    return lax.dot_general(a, b, (((1,), (0,)), ((), ())), precision=HIGHEST, preferred_element_type=F32)


def dot_nt(a, b):
    return lax.dot_general(a, b, (((1,), (1,)), ((), ())), precision=HIGHEST, preferred_element_type=F32)


def kernel(n_x, n_y, ft_in, pt_in, sp_in, ow_in, pro_out, rows_out,
           ft, pt, sp, ow, pro, rows, own, rxl, rxh, ypl, yph, ryl, ryh, pd, rp, pe, ex, yz, fe, cf, mk, ba, bb, ap, wm, acc, xs, ct, pp, orow,
           snd, rcv, in_sem, out_sem, x_send, x_recv, y_send, y_recv, p_send, p_recv, e_send, e_recv):
    gx = lax.axis_index("gx")
    gy = lax.axis_index("gy")
    peer = lambda dx, dy: (lax.rem(gx + (dx + n_x), n_x), lax.rem(gy + (dy + n_y), n_y))

    barrier = pltpu.get_barrier_semaphore()
    far = [j for j in range(1, n_y) if j not in (1, n_y - 1)]
    for dx, dy in AROUND:
        pl.semaphore_signal(barrier, inc=1, device_id=peer(dx, dy), device_id_type=MESH)
    for j in far:
        pl.semaphore_signal(barrier, inc=1, device_id=peer(0, j), device_id_type=MESH)

    loads = [
        pltpu.make_async_copy(src, dst, in_sem.at[i])
        for i, (src, dst) in enumerate(((ft_in, ft), (pt_in, pt), (sp_in, sp), (ow_in, ow)))
    ]
    for copy in loads:
        copy.start()

    zero8 = jnp.zeros((8, 128), F32)

    def clear(x, carry):
        for s in range(8):
            for b in (ba, bb):
                b[s, x, 0:8, :] = zero8
                b[s, x, 32:40, :] = zero8
        for k in range(4):
            fe[k, x, 0:8, :] = zero8
        return carry

    lax.fori_loop(0, E, clear, 0)
    for copy in loads:
        copy.wait()

    pd[...] = jnp.zeros((8, 128), F32)
    for bx in range(2):
        total = None
        for k in range(6):
            place = (iota((16, 128), 1) == iota((16, 128), 0) + 16 * k).astype(F32)
            term = dot(sp[k, bx].astype(F32), place)
            total = term if total is None else total + term
        pd[2 * bx:2 * bx + 2, :] = total

    x_last = gx == n_x - 1
    y_last = gy == n_y - 1
    row16 = iota((16, 128), 0)
    lane16 = iota((16, 128), 1)
    keep_y = jnp.where((row16 == 15) & y_last, 0.0, 1.0)
    keep_z = jnp.where(lane16 == 127, 0.0, 1.0)

    def stage(x, carry):
        keep_x = jnp.where((x == 15) & x_last, 0.0, 1.0)
        p = pt[x]
        px = (p >= 9).astype(jnp.int32) + (p >= 18).astype(jnp.int32)
        q = p - 9 * px
        py = (q >= 3).astype(jnp.int32) + (q >= 6).astype(jnp.int32)
        pz = q - 3 * py
        bx = ((x >> 3) + px + 1) & 1
        by = ((row16 >> 3) + py + 1) & 1
        bz = ((lane16 >> 3) + pz + 1) & 1
        code = (4 * bx + 2 * by + bz).astype(F32)
        values = {FX: ft[0, x] * keep_x, FY: ft[1, x] * keep_y, FZ: ft[2, x] * keep_z, CODE: code}
        for k in range(4):
            own[x * 4 + k] = values[k]
            fe[k, x + 4, 12:28, :] = values[k]
            start = pl.multiple_of(x * 16, 8) + 4 * k
            ypl[pl.ds(start, 4), :] = values[k][0:4]
            yph[pl.ds(start, 4), :] = values[k][12:16]
        return carry

    lax.fori_loop(0, 16, stage, 0)
    pl.semaphore_wait(barrier, 8 + len(far))

    def remote(src, dst, send, recv, dx, dy):
        copy = pltpu.make_async_remote_copy(src_ref=src, dst_ref=dst, send_sem=send, recv_sem=recv,
                                            device_id=peer(dx, dy), device_id_type=MESH)
        copy.start()
        return copy

    pad_copies = [
        remote(pd, rp.at[pl.ds(8 * d, 8)], p_send.at[d], p_recv.at[d], dx, dy) for d, (dx, dy) in enumerate(AROUND)
    ]
    y_copies = [
        remote(yph, ryl.at[pl.ds(64, 256)], y_send.at[0], y_recv.at[0], 0, 1),
        remote(ypl, ryh.at[pl.ds(64, 256)], y_send.at[1], y_recv.at[1], 0, -1),
    ]
    x_copies = [
        remote(own.at[pl.ds(50, 14)], rxl, x_send.at[0], x_recv.at[0], 1, 0),
        remote(own.at[pl.ds(0, 12)], rxh.at[pl.ds(0, 12)], x_send.at[1], x_recv.at[1], -1, 0),
        remote(own.at[pl.ds(15, 1)], rxh.at[pl.ds(12, 1)], x_send.at[2], x_recv.at[2], -1, 0),
        remote(yph.at[pl.ds(192, 64)], ryl.at[pl.ds(0, 64)], y_send.at[2], y_recv.at[2], 1, 1),
        remote(yph.at[pl.ds(0, 64)], ryl.at[pl.ds(320, 64)], y_send.at[3], y_recv.at[3], -1, 1),
        remote(ypl.at[pl.ds(192, 64)], ryh.at[pl.ds(0, 64)], y_send.at[4], y_recv.at[4], 1, -1),
        remote(ypl.at[pl.ds(0, 64)], ryh.at[pl.ds(320, 64)], y_send.at[5], y_recv.at[5], -1, -1),
    ]

    orow[...] = jnp.full((8, 128), -1.0, F32)
    orow[0:1, 0:64] = ow[...].astype(F32)
    owner = jnp.broadcast_to(orow[0:1, :], (128, 128))
    earlier = (owner == owner.T) & (iota((128, 128), 0) < iota((128, 128), 1))
    rank = jnp.sum(earlier.astype(F32), axis=0, keepdims=True)
    target = orow[0:1, :] * 8.0 + rank
    row_f = iota((128, 128), 0).astype(F32)
    for b in range(4):
        shifted = jnp.broadcast_to(target, (8, 128))
        if b:
            shifted = pltpu.roll(shifted, 128 - 16 * b, 1)
        pp[b] = ((row_f == shifted[0:1]) & (iota((128, 128), 1) < 16)).astype(F32)

    c = iota((128, 256), 1)
    up_z, b_x, up_x, b_y, up_y = c >> 7, (c >> 6) & 1, (c >> 5) & 1, (c >> 4) & 1, (c >> 3) & 1
    s_x, s_y, s_z = (c >> 2) & 1, (c >> 1) & 1, c & 1
    o_x = jnp.where(s_x == b_x, 1, 2 * up_x)
    o_y = jnp.where(s_y == b_y, 1, 2 * up_y)
    o_z = jnp.where(s_z == 0, 1, 2 * up_z)
    ct[...] = (iota((128, 256), 0) == (b_x * 2 + b_y) * 32 + 9 * o_x + 3 * o_y + o_z).astype(F32)

    for copy in pad_copies:
        copy.wait_recv()
    low = {-1: 0, 0: 1, 1: 3}
    for dx, dy in AROUND + [(0, 0)]:
        sx, sy = -dx, -dy
        base = 0 if (dx, dy) == (0, 0) else 8 * AROUND.index((dx, dy))
        src = pd if (dx, dy) == (0, 0) else rp
        for i in ((1,) if sx < 0 else (0,) if sx > 0 else (0, 1)):
            for j in ((1,) if sy < 0 else (0,) if sy > 0 else (0, 1)):
                bi = low[sx] + (i if sx == 0 else 0)
                bj = low[sy] + (j if sy == 0 else 0)
                pe[4 * bi + bj:4 * bi + bj + 1, :] = src[base + 2 * i + j:base + 2 * i + j + 1, :]
    block_row = iota((16, 128), 0)
    outside = ((((block_row >> 2) == 0) & (gx == 0)) | (((block_row >> 2) == 3) & x_last)
               | (((block_row & 3) == 0) & (gy == 0)) | (((block_row & 3) == 3) & y_last))
    pads = jnp.where(outside, 0.0, pe[...])
    r_in = iota((128, 128), 0)
    tile_z = (iota((128, 128), 1) + 4) >> 3
    for sz in range(2):
        upper = (tile_z & 1) == sz
        bz = jnp.where(upper, tile_z, tile_z - 1)
        fits = (bz >= 0) & (bz < 16)
        for k in range(5):
            lanes = bz + 16 * k if k < 4 else bz + jnp.where(upper, 64, 80)
            ex[sz * 5 + k] = dot(pads, (fits & (r_in == lanes)).astype(F32))

    row8 = iota((8, 128), 0).astype(F32)
    lane8 = iota((8, 128), 1)
    i_z = ((lane8 + 4) & 7).astype(F32)
    up8 = ((lane8 + 4) >> 3) & 1
    for s in range(8):
        sx, sy, sz = s >> 2, (s >> 1) & 1, s & 1
        for g in range(3):
            bx = g if g % 2 == sx else g - 1
            for t in range(3):
                by = t if t % 2 == sy else t - 1
                r = (bx + 1) * 4 + by + 1
                reach_z = ex[sz * 5 + 4, r:r + 1, :]
                ok_z = jnp.where(up8 == sz, i_z + reach_z, 7.0 - i_z + reach_z) >= 4.0
                if by == t:
                    ok_y = row8 + ex[sz * 5 + 2, r:r + 1, :] >= 4.0
                else:
                    ok_y = row8 <= 3.0 + ex[sz * 5 + 3, r:r + 1, :]
                yz[s, g, 8 * t:8 * t + 8, :] = (ok_z & ok_y).astype(F32)

    def masks(i, carry):
        at = i.astype(F32)
        for s in range(8):
            sx, sy, sz = s >> 2, (s >> 1) & 1, s & 1
            for g in range(3):
                bx = g if g % 2 == sx else g - 1
                for t in range(3):
                    by = t if t % 2 == sy else t - 1
                    r = (bx + 1) * 4 + by + 1
                    if bx == g:
                        ok_x = ex[sz * 5, r:r + 1, :] >= 4.0 - at
                    else:
                        ok_x = ex[sz * 5 + 1, r:r + 1, :] >= at - 3.0
                    mk[s, 8 * g + i, 8 * t:8 * t + 8, :] = jnp.where(ok_x, yz[s, g, 8 * t:8 * t + 8, :], 0.0)
        return carry

    lax.fori_loop(0, 8, masks, 0, unroll=4)

    for copy in y_copies:
        copy.wait_recv()

    def unpack(x):
        for k in range(4):
            start = 16 * x + 4 * k
            if not isinstance(x, int):
                start = pl.multiple_of(x * 16, 8) + 4 * k
            fe[k, x, 8:12, :] = ryl[pl.ds(start, 4), :]
            fe[k, x, 28:32, :] = ryh[pl.ds(start, 4), :]

    def first(x):
        for t in range(3):
            code = fe[CODE, x, 8 + 8 * t:16 + 8 * t, :]
            for s in range(8):
                ba[s, x, 8 + 8 * t:16 + 8 * t, :] = (code == float(s)).astype(F32)

    def coefficients(x):
        for t in range(3):
            a, b = 8 + 8 * t, 16 + 8 * t
            east, west = fe[FX, x, a:b, :], fe[FX, x - 1, a:b, :]
            north, south = fe[FY, x, a:b, :], fe[FY, x, a - 1:b - 1, :]
            top = fe[FZ, x, a:b, :]
            bottom = pltpu.roll(top, 1, 1)
            diagonal = west + east + south + north + bottom + top
            inverse = 1.0 / diagonal
            for i, face in enumerate((east, west, north, south, top, bottom)):
                cf[i, x, 8 * t:8 * t + 8, :] = face * inverse
            cf[6, x, 8 * t:8 * t + 8, :] = diagonal

    def around(src, s, x, t, faces):
        east, west, north, south, top, bottom = faces
        a, b = 8 + 8 * t, 16 + 8 * t
        centre = src[s, x, a:b, :]
        total = (east * src[s, x + 1, a:b, :] + west * src[s, x - 1, a:b, :]
                 + north * src[s, x, a + 1:b + 1, :] + south * src[s, x, a - 1:b - 1, :]
                 + top * pltpu.roll(centre, 127, 1) + bottom * pltpu.roll(centre, 1, 1))
        return centre, total

    def smooth(src, dst, x):
        for t in range(3):
            faces = [cf[i, x, 8 * t:8 * t + 8, :] for i in range(6)]
            updated = []
            for s in range(8):
                centre, total = around(src, s, x, t, faces)
                updated.append(mk[s, x, 8 * t:8 * t + 8, :] * (0.5 * centre + total))
            whole = ((updated[0] + updated[1]) + (updated[2] + updated[3])) + (
                (updated[4] + updated[5]) + (updated[6] + updated[7]))
            scale = 1.0 / jnp.where(whole > 0.0, whole, 1.0)
            for s in range(8):
                dst[s, x, 8 + 8 * t:16 + 8 * t, :] = updated[s] * scale

    def apply(x):
        for t in range(3):
            faces = [cf[i, x, 8 * t:8 * t + 8, :] for i in range(6)]
            diagonal = cf[6, x, 8 * t:8 * t + 8, :]
            for s in range(8):
                centre, total = around(ba, s, x, t, faces)
                ap[s, x, 8 * t:8 * t + 8, :] = diagonal * (centre - total)

    def weigh(a):
        for i in range(5):
            x = SUM_START[a] + 4 + i
            for t in range(3):
                code = fe[CODE, x, 8 + 8 * t:16 + 8 * t, :].astype(jnp.int32)
                in_x = (((code >> 2) & 1) == a // 2).astype(F32)
                odd_y = ((code >> 1) & 1).astype(F32)
                odd_z = (code & 1).astype(F32)
                in_y = 1.0 - odd_y if t == 0 else odd_y
                wm[a * 5 + i, 0, 8 * t:8 * t + 8, :] = in_x
                wm[a * 5 + i, 1, 8 * t:8 * t + 8, :] = in_x * odd_z
                wm[a * 5 + i, 2, 8 * t:8 * t + 8, :] = in_x * in_y
                wm[a * 5 + i, 3, 8 * t:8 * t + 8, :] = in_x * in_y * odd_z

    def sums(a, s):
        for t in range(3):
            parts = [None] * 4
            for i in range(5):
                value = ap[s, SUM_START[a] + 4 + i, 8 * t:8 * t + 8, :]
                for m in range(4) if t == 1 else (2, 3):
                    if m == 0 and i not in SUM_MASKED[a]:
                        term = value
                    else:
                        term = value * wm[a * 5 + i, m, 8 * t:8 * t + 8, :]
                    parts[m] = term if parts[m] is None else parts[m] + term
            for m in range(4) if t == 1 else (2, 3):
                place = a * 8 + (m - 2 if t == 0 else m + 2 if t == 1 else m + 4)
                acc[pl.ds(pl.multiple_of((place * 8 + s) * 8, 8), 8), :] = parts[m]

    def over_rows(a):
        r = []
        for place in range(a * 8, a * 8 + 8):
            total = acc[pl.ds(place * 64, 8, stride=8), :]
            for y in range(1, 8):
                total = total + acc[pl.ds(place * 64 + y, 8, stride=8), :]
            r.append(total)
        r[2], r[3] = r[2] - r[4], r[3] - r[5]
        for b in range(4):
            for m in range(2):
                start = m * 128 + (a * 4 + b) * 8
                xs[start:start + 8, :] = r[2 * b + m]

    def layers(step, start, stop, unroll):
        def body(x, carry):
            step(x)
            return carry

        lax.fori_loop(start, stop, body, 0, unroll=unroll)

    def both(step, start, other, count, unroll):
        def body(i, carry):
            step(start + i)
            step(other + i)
            return carry

        lax.fori_loop(0, count, body, 0, unroll=unroll)

    def give(x):
        for s in range(8):
            pro[s, x] = ba[s, x + 4, 12:28, :]

    once = functools.partial(smooth, ba, bb)
    twice = functools.partial(smooth, bb, ba)

    layers(unpack, 4, 20, 8)
    layers(first, 4, 20, 8)
    layers(coefficients, 5, 20, 5)
    layers(once, 5, 19, 7)
    layers(twice, 6, 18, 6)
    layers(give, 2, 14, 4)
    layers(apply, 7, 17, 5)
    weigh(1)
    weigh(2)
    layers(functools.partial(sums, 1), 0, 8, 4)
    layers(functools.partial(sums, 2), 0, 8, 4)

    for copy in x_copies:
        copy.wait_recv()
    for i in range(14):
        flat = 50 + i
        fe[flat % 4, flat // 4 - 12, 12:28, :] = rxl[i]
    for i in range(12):
        fe[i % 4, 20 + i // 4, 12:28, :] = rxh[i]
    fe[CODE, 23, 12:28, :] = rxh[12]
    for x in range(4):
        unpack(x)
        unpack(20 + x)
    both(first, 0, 20, 4, 4)
    layers(coefficients, 1, 5, 4)
    layers(coefficients, 20, 23, 3)
    both(once, 1, 19, 4, 4)
    both(twice, 2, 18, 4, 4)
    both(give, 0, 14, 2, 2)
    write = pltpu.make_async_copy(pro, pro_out, out_sem.at[0])
    write.start()
    both(apply, 3, 17, 4, 4)
    weigh(0)
    weigh(3)
    layers(functools.partial(sums, 0), 0, 8, 4)
    layers(functools.partial(sums, 3), 0, 8, 4)
    for a in range(4):
        over_rows(a)

    lane_tile = (iota((128, 128), 0) + 4) >> 3
    col = iota((128, 128), 1)
    even = (col & 1) == 0
    even_row = (iota((128, 128), 0) & 1) == 0
    halves = []
    for up in range(2):
        gather = ((lane_tile == col + up) & (col < 16)).astype(F32)
        z = dot(xs[...], gather)
        v = jnp.where(even, z[0:128] - z[128:256], z[128:256])
        other = jnp.where(even_row, pltpu.roll(v, 127, 0), pltpu.roll(v, 1, 0))
        halves.append(jnp.where(even, v, other))
    entries = dot(ct[:, 0:128], halves[0]) + dot(ct[:, 128:256], halves[1])
    routed = dot_nt(pp[0], entries[0:32])
    for b in range(1, 4):
        routed = routed + dot_nt(pp[b], entries[32 * b:32 * b + 32])
    snd[:, 0:32] = routed
    snd[:, 32:128] = jnp.zeros((128, 96), F32)

    mine = pl.multiple_of(gy * 8, 8)
    sent = []
    for j in range(1, n_y):
        there = lax.rem(gy + j, n_y)
        sent.append(remote(snd.at[pl.ds(pl.multiple_of(there * 8, 8), 8)], rcv.at[pl.ds(mine, 8)],
                           e_send.at[j], e_recv.at[j], 0, j))
    rcv[pl.ds(mine, 8), :] = snd[pl.ds(mine, 8), :]
    for copy in sent:
        copy.wait_recv()
    rows[...] = rcv[...].T[0:27, :]
    write_rows = pltpu.make_async_copy(rows, rows_out, out_sem.at[1])
    write_rows.start()
    write.wait()
    write_rows.wait()
    for copy in pad_copies + y_copies + x_copies + sent:
        copy.wait_send()


def solution(mesh):
    n_x, n_y = mesh.shape["gx"], mesh.shape["gy"]
    hbm = pl.BlockSpec(memory_space=pltpu.HBM)
    dma = pltpu.SemaphoreType.DMA

    def on_device(face_trans, partition, support_pad, owners):
        prolongation, rows = pl.pallas_call(
            functools.partial(kernel, n_x, n_y),
            out_shape=(
                jax.ShapeDtypeStruct((8, 16, 16, 128), F32),
                jax.ShapeDtypeStruct((27, 128), F32),
            ),
            in_specs=[hbm] * 4,
            out_specs=(hbm, hbm),
            scratch_shapes=[
                pltpu.VMEM((3, 16, 16, 128), F32),
                pltpu.VMEM((16, 16, 128), jnp.int32),
                pltpu.VMEM((6, 2, 2, 16), jnp.int32),
                pltpu.VMEM((1, 64), jnp.int32),
                pltpu.VMEM((8, 16, 16, 128), F32),
                pltpu.VMEM((27, 128), F32),
                pltpu.VMEM((64, 16, 128), F32),
                pltpu.VMEM((14, 16, 128), F32),
                pltpu.VMEM((13, 16, 128), F32),
                pltpu.VMEM((256, 128), F32),
                pltpu.VMEM((256, 128), F32),
                pltpu.VMEM((384, 128), F32),
                pltpu.VMEM((384, 128), F32),
                pltpu.VMEM((8, 128), F32),
                pltpu.VMEM((64, 128), F32),
                pltpu.VMEM((16, 128), F32),
                pltpu.VMEM((10, 16, 128), F32),
                pltpu.VMEM((8, 3, E, 128), F32),
                pltpu.VMEM((4, E, 40, 128), F32),
                pltpu.VMEM((7, E, E, 128), F32),
                pltpu.VMEM((8, E, E, 128), F32),
                pltpu.VMEM((8, E, 40, 128), F32),
                pltpu.VMEM((8, E, 40, 128), F32),
                pltpu.VMEM((8, E, E, 128), F32),
                pltpu.VMEM((20, 4, E, 128), F32),
                pltpu.VMEM((2048, 128), F32),
                pltpu.VMEM((256, 128), F32),
                pltpu.VMEM((128, 256), F32),
                pltpu.VMEM((4, 128, 128), F32),
                pltpu.VMEM((8, 128), F32),
                pltpu.VMEM((128, 128), F32),
                pltpu.VMEM((8 * n_y, 128), F32),
                dma((4,)), dma((2,)), dma((3,)), dma((3,)), dma((6,)), dma((6,)), dma((8,)), dma((8,)), dma((n_y,)), dma((n_y,)),
            ],
            compiler_params=pltpu.CompilerParams(
                collective_id=0, has_side_effects=True, vmem_limit_bytes=60 * 2**20
            ),
        )(face_trans, partition, support_pad, owners.reshape(1, 64))
        return prolongation, rows.reshape(1, 1, 27, 128)

    placed = (
        P(None, "gx", "gy", None),
        P("gx", "gy", None),
        P(None, "gx", "gy", None),
        P("gx", "gy", None, None),
    )
    return jax.shard_map(
        on_device,
        mesh=mesh,
        in_specs=placed,
        out_specs=(P(None, "gx", "gy", None), P("gx", "gy", None, None)),
        check_vma=False,
    )
```

```python
import functools

import jax
import jax.numpy as jnp
from jax import lax
from jax.experimental import pallas as pl
from jax.experimental.pallas import tpu as pltpu
from jax.sharding import PartitionSpec as P

MESH = pl.DeviceIdType.MESH
F32 = jnp.float32
HIGHEST = lax.Precision.HIGHEST

E = 24
FY, FZ, FX, CODE = range(4)
AROUND = [(dx, dy) for dx in (-1, 0, 1) for dy in (-1, 0, 1) if (dx, dy) != (0, 0)]
SUM_START = (-1, 4, 7, 12)
SUM_MASKED = ((0, 1), (3, 4), (0, 1), (3, 4))


def iota(shape, dim):
    return lax.broadcasted_iota(jnp.int32, shape, dim)


def dot(a, b):
    return lax.dot_general(a, b, (((1,), (0,)), ((), ())), precision=HIGHEST, preferred_element_type=F32)


def dot_nt(a, b):
    return lax.dot_general(a, b, (((1,), (1,)), ((), ())), precision=HIGHEST, preferred_element_type=F32)


def kernel(n_x, n_y, ft_in, pt_in, sp_in, ow_in, pro, rows,
           ft, pt, sp, ow, own, rxl, rxh, ypl, yph, ryl, ryh, pd, rp, pe, ex, yz, fe, cf, mk, ba, bb, ap, wm, acc, xs, ct, pp, orow,
           snd, rcv, in_sem, x_send, x_recv, y_send, y_recv, p_send, p_recv, e_send, e_recv):
    gx = lax.axis_index("gx")
    gy = lax.axis_index("gy")
    peer = lambda dx, dy: (lax.rem(gx + (dx + n_x), n_x), lax.rem(gy + (dy + n_y), n_y))

    barrier = pltpu.get_barrier_semaphore()
    far = [j for j in range(1, n_y) if j not in (1, n_y - 1)]

    def inside(dx, dy):
        fits = None
        for d, at, count in ((dx, gx, n_x), (dy, gy, n_y)):
            if d:
                part = at > 0 if d < 0 else at < count - 1
                fits = part if fits is None else fits & part
        return fits

    for dx, dy in AROUND:
        def greet(dx=dx, dy=dy):
            pl.semaphore_signal(barrier, inc=1, device_id=peer(dx, dy), device_id_type=MESH)

        if dx == 0:
            greet()
        else:
            pl.when(inside(dx, dy))(greet)
    for j in far:
        pl.semaphore_signal(barrier, inc=1, device_id=peer(0, j), device_id_type=MESH)

    loads = [
        pltpu.make_async_copy(src, dst, in_sem.at[i])
        for i, (src, dst) in enumerate(((ft_in, ft), (pt_in, pt), (sp_in, sp), (ow_in, ow)))
    ]
    for copy in loads:
        copy.start()

    zero8 = jnp.zeros((8, 128), F32)

    def clear(x, carry):
        for s in range(8):
            for b in (ba, bb):
                b[s, x, 0:8, :] = zero8
                b[s, x, 32:40, :] = zero8
        for k in range(4):
            fe[k, x, 0:8, :] = zero8
        return carry

    lax.fori_loop(0, E, clear, 0)
    for copy in loads:
        copy.wait()

    pd[...] = jnp.zeros((8, 128), F32)
    for bx in range(2):
        total = None
        for k in range(6):
            place = (iota((16, 128), 1) == iota((16, 128), 0) + 16 * k).astype(F32)
            term = dot(sp[k, bx].astype(F32), place)
            total = term if total is None else total + term
        pd[2 * bx:2 * bx + 2, :] = total

    x_last = gx == n_x - 1
    y_last = gy == n_y - 1
    row16 = iota((16, 128), 0)
    lane16 = iota((16, 128), 1)
    keep_y = jnp.where((row16 == 15) & y_last, 0.0, 1.0)
    keep_z = jnp.where(lane16 == 127, 0.0, 1.0)

    def stage(x, carry):
        keep_x = jnp.where((x == 15) & x_last, 0.0, 1.0)
        p = pt[x]
        px = (p >= 9).astype(jnp.int32) + (p >= 18).astype(jnp.int32)
        q = p - 9 * px
        py = (q >= 3).astype(jnp.int32) + (q >= 6).astype(jnp.int32)
        pz = q - 3 * py
        bx = ((x >> 3) + px + 1) & 1
        by = ((row16 >> 3) + py + 1) & 1
        bz = ((lane16 >> 3) + pz + 1) & 1
        code = (4 * bx + 2 * by + bz).astype(F32)
        values = {FX: ft[0, x] * keep_x, FY: ft[1, x] * keep_y, FZ: ft[2, x] * keep_z, CODE: code}
        for k in range(4):
            own[x * 4 + k] = values[k]
            fe[k, x + 4, 12:28, :] = values[k]
            start = pl.multiple_of(x * 16, 8) + 4 * k
            ypl[pl.ds(start, 4), :] = values[k][0:4]
            yph[pl.ds(start, 4), :] = values[k][12:16]
        return carry

    lax.fori_loop(0, 16, stage, 0)
    sides_x = 2 - (gx == 0).astype(jnp.int32) - x_last.astype(jnp.int32)
    sides_y = 2 - (gy == 0).astype(jnp.int32) - y_last.astype(jnp.int32)
    pl.semaphore_wait(barrier, 2 + len(far) + sides_x * (1 + sides_y))

    def remote(src, dst, send, recv, dx, dy):
        return pltpu.make_async_remote_copy(src_ref=src, dst_ref=dst, send_sem=send, recv_sem=recv,
                                            device_id=peer(dx, dy), device_id_type=MESH)

    def between(act, copies, sign=1):
        for (dx, dy), copy in copies:
            pl.when(inside(sign * dx, sign * dy))(functools.partial(act, copy))

    def start(copies):
        between(lambda copy: copy.start(), copies)

    def arrive(copies):
        between(lambda copy: copy.wait_recv(), copies, -1)

    def leave(copies):
        between(lambda copy: copy.wait_send(), copies)

    def link(src, dst, send, recv, dx, dy):
        return (dx, dy), remote(src, dst, send, recv, dx, dy)

    pad_copies = [
        link(pd, rp.at[pl.ds(8 * d, 8)], p_send.at[d], p_recv.at[d], dx, dy) for d, (dx, dy) in enumerate(AROUND)
    ]
    y_copies = [
        link(yph, ryl.at[pl.ds(64, 256)], y_send.at[0], y_recv.at[0], 0, 1),
        link(ypl, ryh.at[pl.ds(64, 256)], y_send.at[1], y_recv.at[1], 0, -1),
    ]
    x_copies = [
        link(own.at[pl.ds(50, 14)], rxl, x_send.at[0], x_recv.at[0], 1, 0),
        link(own.at[pl.ds(0, 12)], rxh.at[pl.ds(0, 12)], x_send.at[1], x_recv.at[1], -1, 0),
        link(own.at[pl.ds(15, 1)], rxh.at[pl.ds(12, 1)], x_send.at[2], x_recv.at[2], -1, 0),
        link(yph.at[pl.ds(192, 64)], ryl.at[pl.ds(0, 64)], y_send.at[2], y_recv.at[2], 1, 1),
        link(yph.at[pl.ds(0, 64)], ryl.at[pl.ds(320, 64)], y_send.at[3], y_recv.at[3], -1, 1),
        link(ypl.at[pl.ds(192, 64)], ryh.at[pl.ds(0, 64)], y_send.at[4], y_recv.at[4], 1, -1),
        link(ypl.at[pl.ds(0, 64)], ryh.at[pl.ds(320, 64)], y_send.at[5], y_recv.at[5], -1, -1),
    ]

    start(x_copies[:3])
    start(pad_copies)
    start(y_copies)
    start(x_copies[3:])

    def beyond(ref, layers_of_x, code):
        for x in layers_of_x:
            ref[16 * x:16 * x + 16, :] = jnp.ones((16, 128), F32)
            ref[16 * x + 4 * CODE:16 * x + 4 * CODE + 4, :] = jnp.full((4, 128), code, F32)

    def closed_west():
        for r in (ryl, ryh):
            r[48 + 4 * FX:52 + 4 * FX, :] = jnp.zeros((4, 128), F32)

    @pl.when(gx == 0)
    def _():
        for i in range(14):
            k = (50 + i) % 4
            rxl[i] = jnp.full((16, 128), 6.0 if k == CODE else 0.0 if (k, i) == (FX, 12) else 1.0, F32)
        beyond(ryl, range(4), 6.0)
        beyond(ryh, range(4), 6.0)
        closed_west()

    @pl.when(x_last)
    def _():
        rxh[...] = jnp.ones_like(rxh)
        beyond(ryl, range(20, 24), 1.0)
        beyond(ryh, range(20, 24), 1.0)

    @pl.when(gy == 0)
    def _():
        beyond(ryl, range(E), 6.0)
        for x in range(E):
            ryl[16 * x + 4 * FY + 3:16 * x + 4 * FY + 4, :] = jnp.zeros((1, 128), F32)
        pl.when(gx == 0)(closed_west)

    @pl.when(y_last)
    def _():
        beyond(ryh, range(E), 1.0)
        pl.when(gx == 0)(closed_west)

    orow[...] = jnp.full((8, 128), -1.0, F32)
    orow[0:1, 0:64] = ow[...].astype(F32)
    owner = jnp.broadcast_to(orow[0:1, :], (128, 128))
    earlier = (owner == owner.T) & (iota((128, 128), 0) < iota((128, 128), 1))
    rank = jnp.sum(earlier.astype(F32), axis=0, keepdims=True)
    target = orow[0:1, :] * 8.0 + rank
    row_f = iota((128, 128), 0).astype(F32)
    for b in range(4):
        shifted = jnp.broadcast_to(target, (8, 128))
        if b:
            shifted = pltpu.roll(shifted, 128 - 16 * b, 1)
        pp[b] = ((row_f == shifted[0:1]) & (iota((128, 128), 1) < 16)).astype(F32)

    c = iota((128, 256), 1)
    up_z, b_x, up_x, b_y, up_y = c >> 7, (c >> 6) & 1, (c >> 5) & 1, (c >> 4) & 1, (c >> 3) & 1
    s_x, s_y, s_z = (c >> 2) & 1, (c >> 1) & 1, c & 1
    o_x = jnp.where(s_x == b_x, 1, 2 * up_x)
    o_y = jnp.where(s_y == b_y, 1, 2 * up_y)
    o_z = jnp.where(s_z == 0, 1, 2 * up_z)
    ct[...] = (iota((128, 256), 0) == (b_x * 2 + b_y) * 32 + 9 * o_x + 3 * o_y + o_z).astype(F32)

    arrive(pad_copies)
    low = {-1: 0, 0: 1, 1: 3}
    for dx, dy in AROUND + [(0, 0)]:
        sx, sy = -dx, -dy
        base = 0 if (dx, dy) == (0, 0) else 8 * AROUND.index((dx, dy))
        src = pd if (dx, dy) == (0, 0) else rp
        for i in ((1,) if sx < 0 else (0,) if sx > 0 else (0, 1)):
            for j in ((1,) if sy < 0 else (0,) if sy > 0 else (0, 1)):
                bi = low[sx] + (i if sx == 0 else 0)
                bj = low[sy] + (j if sy == 0 else 0)
                pe[4 * bi + bj:4 * bi + bj + 1, :] = src[base + 2 * i + j:base + 2 * i + j + 1, :]
    block_row = iota((16, 128), 0)
    outside = ((((block_row >> 2) == 0) & (gx == 0)) | (((block_row >> 2) == 3) & x_last)
               | (((block_row & 3) == 0) & (gy == 0)) | (((block_row & 3) == 3) & y_last))
    pads = jnp.where(outside, 0.0, pe[...])
    r_in = iota((128, 128), 0)
    tile_z = (iota((128, 128), 1) + 4) >> 3
    for sz in range(2):
        upper = (tile_z & 1) == sz
        bz = jnp.where(upper, tile_z, tile_z - 1)
        fits = (bz >= 0) & (bz < 16)
        for k in range(5):
            lanes = bz + 16 * k if k < 4 else bz + jnp.where(upper, 64, 80)
            ex[sz * 5 + k] = dot(pads, (fits & (r_in == lanes)).astype(F32))

    row8 = iota((8, 128), 0).astype(F32)
    lane8 = iota((8, 128), 1)
    i_z = ((lane8 + 4) & 7).astype(F32)
    up8 = ((lane8 + 4) >> 3) & 1
    for s in range(8):
        sx, sy, sz = s >> 2, (s >> 1) & 1, s & 1
        for g in range(3):
            bx = g if g % 2 == sx else g - 1
            for t in range(3):
                by = t if t % 2 == sy else t - 1
                r = (bx + 1) * 4 + by + 1
                reach_z = ex[sz * 5 + 4, r:r + 1, :]
                ok_z = jnp.where(up8 == sz, i_z + reach_z, 7.0 - i_z + reach_z) >= 4.0
                if by == t:
                    ok_y = row8 + ex[sz * 5 + 2, r:r + 1, :] >= 4.0
                else:
                    ok_y = row8 <= 3.0 + ex[sz * 5 + 3, r:r + 1, :]
                yz[s, g, 8 * t:8 * t + 8, :] = (ok_z & ok_y).astype(F32)

    def masks(i, carry):
        at = i.astype(F32)
        for s in range(8):
            sx, sy, sz = s >> 2, (s >> 1) & 1, s & 1
            for g in range(3):
                bx = g if g % 2 == sx else g - 1
                for t in range(3):
                    by = t if t % 2 == sy else t - 1
                    r = (bx + 1) * 4 + by + 1
                    if bx == g:
                        ok_x = ex[sz * 5, r:r + 1, :] >= 4.0 - at
                    else:
                        ok_x = ex[sz * 5 + 1, r:r + 1, :] >= at - 3.0
                    mk[s, 8 * g + i, 8 * t:8 * t + 8, :] = jnp.where(ok_x, yz[s, g, 8 * t:8 * t + 8, :], 0.0)
        return carry

    lax.fori_loop(0, 8, masks, 0, unroll=4)

    arrive(y_copies)

    def unpack(x):
        for k in range(4):
            start = 16 * x + 4 * k
            if not isinstance(x, int):
                start = pl.multiple_of(x * 16, 8) + 4 * k
            fe[k, x, 8:12, :] = ryl[pl.ds(start, 4), :]
            fe[k, x, 28:32, :] = ryh[pl.ds(start, 4), :]

    def first(x):
        for t in range(3):
            code = fe[CODE, x, 8 + 8 * t:16 + 8 * t, :]
            for s in range(8):
                ba[s, x, 8 + 8 * t:16 + 8 * t, :] = (code == float(s)).astype(F32)

    def coefficients(x):
        for t in range(3):
            a, b = 8 + 8 * t, 16 + 8 * t
            east, west = fe[FX, x, a:b, :], fe[FX, x - 1, a:b, :]
            north, south = fe[FY, x, a:b, :], fe[FY, x, a - 1:b - 1, :]
            top = fe[FZ, x, a:b, :]
            bottom = pltpu.roll(top, 1, 1)
            diagonal = west + east + south + north + bottom + top
            inverse = 1.0 / diagonal
            for i, face in enumerate((east, west, north, south, top, bottom)):
                cf[i, x, 8 * t:8 * t + 8, :] = face * inverse
            cf[6, x, 8 * t:8 * t + 8, :] = diagonal

    def around(src, s, x, t, faces):
        east, west, north, south, top, bottom = faces
        a, b = 8 + 8 * t, 16 + 8 * t
        centre = src[s, x, a:b, :]
        total = (east * src[s, x + 1, a:b, :] + west * src[s, x - 1, a:b, :]
                 + north * src[s, x, a + 1:b + 1, :] + south * src[s, x, a - 1:b - 1, :]
                 + top * pltpu.roll(centre, 127, 1) + bottom * pltpu.roll(centre, 1, 1))
        return centre, total

    def smooth(src, dst, x):
        for t in range(3):
            faces = [cf[i, x, 8 * t:8 * t + 8, :] for i in range(6)]
            updated = []
            for s in range(8):
                centre, total = around(src, s, x, t, faces)
                updated.append(mk[s, x, 8 * t:8 * t + 8, :] * (0.5 * centre + total))
            whole = ((updated[0] + updated[1]) + (updated[2] + updated[3])) + (
                (updated[4] + updated[5]) + (updated[6] + updated[7]))
            scale = 1.0 / jnp.where(whole > 0.0, whole, 1.0)
            for s in range(8):
                dst[s, x, 8 + 8 * t:16 + 8 * t, :] = updated[s] * scale

    def apply(x):
        for t in range(3):
            faces = [cf[i, x, 8 * t:8 * t + 8, :] for i in range(6)]
            diagonal = cf[6, x, 8 * t:8 * t + 8, :]
            for s in range(8):
                centre, total = around(ba, s, x, t, faces)
                ap[s, x, 8 * t:8 * t + 8, :] = diagonal * (centre - total)

    def weigh(a):
        for i in range(5):
            x = SUM_START[a] + 4 + i
            for t in range(3):
                code = fe[CODE, x, 8 + 8 * t:16 + 8 * t, :].astype(jnp.int32)
                in_x = (((code >> 2) & 1) == a // 2).astype(F32)
                odd_y = ((code >> 1) & 1).astype(F32)
                odd_z = (code & 1).astype(F32)
                in_y = 1.0 - odd_y if t == 0 else odd_y
                wm[a * 5 + i, 0, 8 * t:8 * t + 8, :] = in_x
                wm[a * 5 + i, 1, 8 * t:8 * t + 8, :] = in_x * odd_z
                wm[a * 5 + i, 2, 8 * t:8 * t + 8, :] = in_x * in_y
                wm[a * 5 + i, 3, 8 * t:8 * t + 8, :] = in_x * in_y * odd_z

    def sums(a, s):
        for t in range(3):
            parts = [None] * 4
            for i in range(5):
                value = ap[s, SUM_START[a] + 4 + i, 8 * t:8 * t + 8, :]
                for m in range(4) if t == 1 else (2, 3):
                    if m == 0 and i not in SUM_MASKED[a]:
                        term = value
                    else:
                        term = value * wm[a * 5 + i, m, 8 * t:8 * t + 8, :]
                    parts[m] = term if parts[m] is None else parts[m] + term
            for m in range(4) if t == 1 else (2, 3):
                place = a * 8 + (m - 2 if t == 0 else m + 2 if t == 1 else m + 4)
                acc[pl.ds(pl.multiple_of((place * 8 + s) * 8, 8), 8), :] = parts[m]

    def over_rows(a):
        r = []
        for place in range(a * 8, a * 8 + 8):
            total = acc[pl.ds(place * 64, 8, stride=8), :]
            for y in range(1, 8):
                total = total + acc[pl.ds(place * 64 + y, 8, stride=8), :]
            r.append(total)
        r[2], r[3] = r[2] - r[4], r[3] - r[5]
        for b in range(4):
            for m in range(2):
                start = m * 128 + (a * 4 + b) * 8
                xs[start:start + 8, :] = r[2 * b + m]

    def layers(step, start, stop, unroll):
        def body(x, carry):
            step(x)
            return carry

        lax.fori_loop(start, stop, body, 0, unroll=unroll)

    def both(step, start, other, count, unroll):
        def body(i, carry):
            step(start + i)
            step(other + i)
            return carry

        lax.fori_loop(0, count, body, 0, unroll=unroll)

    def give(x):
        for s in range(8):
            pro[s, x] = ba[s, x + 4, 12:28, :]

    once = functools.partial(smooth, ba, bb)
    twice = functools.partial(smooth, bb, ba)

    layers(unpack, 4, 20, 8)
    layers(first, 4, 20, 8)
    layers(coefficients, 5, 20, 5)
    layers(once, 5, 19, 7)
    layers(twice, 6, 18, 6)
    layers(give, 2, 14, 4)
    layers(apply, 7, 17, 5)
    weigh(1)
    weigh(2)
    layers(functools.partial(sums, 1), 0, 8, 4)
    layers(functools.partial(sums, 2), 0, 8, 4)

    arrive(x_copies)
    for i in range(14):
        flat = 50 + i
        fe[flat % 4, flat // 4 - 12, 12:28, :] = rxl[i]
    for i in range(12):
        fe[i % 4, 20 + i // 4, 12:28, :] = rxh[i]
    fe[CODE, 23, 12:28, :] = rxh[12]
    for x in range(4):
        unpack(x)
        unpack(20 + x)
    both(first, 0, 20, 4, 4)
    layers(coefficients, 1, 5, 4)
    layers(coefficients, 20, 23, 3)
    both(once, 1, 19, 4, 4)
    both(twice, 2, 18, 4, 4)
    both(give, 0, 14, 2, 2)
    both(apply, 3, 17, 4, 4)
    weigh(0)
    weigh(3)
    layers(functools.partial(sums, 0), 0, 8, 4)
    layers(functools.partial(sums, 3), 0, 8, 4)
    for a in range(4):
        over_rows(a)

    lane_tile = (iota((128, 128), 0) + 4) >> 3
    col = iota((128, 128), 1)
    even = (col & 1) == 0
    even_row = (iota((128, 128), 0) & 1) == 0
    halves = []
    for up in range(2):
        gather = ((lane_tile == col + up) & (col < 16)).astype(F32)
        z = dot(xs[...], gather)
        v = jnp.where(even, z[0:128] - z[128:256], z[128:256])
        other = jnp.where(even_row, pltpu.roll(v, 127, 0), pltpu.roll(v, 1, 0))
        halves.append(jnp.where(even, v, other))
    entries = dot(ct[:, 0:128], halves[0]) + dot(ct[:, 128:256], halves[1])
    routed = dot_nt(pp[0], entries[0:32])
    for b in range(1, 4):
        routed = routed + dot_nt(pp[b], entries[32 * b:32 * b + 32])
    snd[:, 0:32] = routed
    snd[:, 32:128] = jnp.zeros((128, 96), F32)

    mine = pl.multiple_of(gy * 8, 8)
    sent = []
    for j in range(1, n_y):
        there = lax.rem(gy + j, n_y)
        copy = remote(snd.at[pl.ds(pl.multiple_of(there * 8, 8), 8)], rcv.at[pl.ds(mine, 8)],
                      e_send.at[j], e_recv.at[j], 0, j)
        copy.start()
        sent.append(copy)
    rcv[pl.ds(mine, 8), :] = snd[pl.ds(mine, 8), :]
    for copy in sent:
        copy.wait_recv()
    rows[:, 0, :] = rcv[...].T[0:27, :]
    leave(pad_copies + y_copies + x_copies)
    for copy in sent:
        copy.wait_send()


def writer(pro, rows, pro_out, rows_out, sem):
    copies = [pltpu.make_async_copy(pro, pro_out, sem.at[0]), pltpu.make_async_copy(rows, rows_out, sem.at[1])]
    for copy in copies:
        copy.start()
    for copy in copies:
        copy.wait()


def solution(mesh):
    n_x, n_y = mesh.shape["gx"], mesh.shape["gy"]
    hbm = pl.BlockSpec(memory_space=pltpu.HBM)
    vmem = pl.BlockSpec(memory_space=pltpu.VMEM)
    dma = pltpu.SemaphoreType.DMA

    def on_device(face_trans, partition, support_pad, owners):
        prolongation, rows = pl.pallas_call(
            functools.partial(kernel, n_x, n_y),
            out_shape=(
                pltpu.VMEM((8, 16, 16, 128), F32),
                pltpu.VMEM((27, 1, 128), F32),
            ),
            in_specs=[hbm] * 4,
            out_specs=(vmem, vmem),
            scratch_shapes=[
                pltpu.VMEM((3, 16, 16, 128), F32),
                pltpu.VMEM((16, 16, 128), jnp.int32),
                pltpu.VMEM((6, 2, 2, 16), jnp.int32),
                pltpu.VMEM((1, 64), jnp.int32),
                pltpu.VMEM((64, 16, 128), F32),
                pltpu.VMEM((14, 16, 128), F32),
                pltpu.VMEM((13, 16, 128), F32),
                pltpu.VMEM((256, 128), F32),
                pltpu.VMEM((256, 128), F32),
                pltpu.VMEM((384, 128), F32),
                pltpu.VMEM((384, 128), F32),
                pltpu.VMEM((8, 128), F32),
                pltpu.VMEM((64, 128), F32),
                pltpu.VMEM((16, 128), F32),
                pltpu.VMEM((10, 16, 128), F32),
                pltpu.VMEM((8, 3, E, 128), F32),
                pltpu.VMEM((4, E, 40, 128), F32),
                pltpu.VMEM((7, E, E, 128), F32),
                pltpu.VMEM((8, E, E, 128), F32),
                pltpu.VMEM((8, E, 40, 128), F32),
                pltpu.VMEM((8, E, 40, 128), F32),
                pltpu.VMEM((8, E, E, 128), F32),
                pltpu.VMEM((20, 4, E, 128), F32),
                pltpu.VMEM((2048, 128), F32),
                pltpu.VMEM((256, 128), F32),
                pltpu.VMEM((128, 256), F32),
                pltpu.VMEM((4, 128, 128), F32),
                pltpu.VMEM((8, 128), F32),
                pltpu.VMEM((128, 128), F32),
                pltpu.VMEM((8 * n_y, 128), F32),
                dma((4,)), dma((3,)), dma((3,)), dma((6,)), dma((6,)), dma((8,)), dma((8,)), dma((n_y,)), dma((n_y,)),
            ],
            compiler_params=pltpu.CompilerParams(
                collective_id=0, has_side_effects=True, vmem_limit_bytes=48 * 2**20
            ),
        )(*(pltpu.with_memory_space_constraint(a, pltpu.HBM)
            for a in (face_trans, partition, support_pad, owners.reshape(1, 64))))
        prolongation, rows = pl.pallas_call(
            writer,
            out_shape=(
                jax.ShapeDtypeStruct((8, 16, 16, 128), F32),
                jax.ShapeDtypeStruct((27, 1, 128), F32),
            ),
            in_specs=[vmem] * 2,
            out_specs=(hbm, hbm),
            scratch_shapes=[dma((2,))],
        )(*(pltpu.with_memory_space_constraint(a, pltpu.VMEM) for a in (prolongation, rows)))
        return prolongation, rows.reshape(1, 1, 27, 128)

    placed = (
        P(None, "gx", "gy", None),
        P("gx", "gy", None),
        P(None, "gx", "gy", None),
        P("gx", "gy", None, None),
    )
    return jax.shard_map(
        on_device,
        mesh=mesh,
        in_specs=placed,
        out_specs=(P(None, "gx", "gy", None), P("gx", "gy", None, None)),
        check_vma=False,
    )
```

```python
import functools

import jax
import jax.numpy as jnp
from jax import lax
from jax.experimental import pallas as pl
from jax.experimental.pallas import tpu as pltpu
from jax.sharding import PartitionSpec as P

MESH = pl.DeviceIdType.MESH
F32 = jnp.float32
HIGHEST = lax.Precision.HIGHEST

E = 24
FY, FZ, FX, CODE = range(4)
AROUND = [(dx, dy) for dx in (-1, 0, 1) for dy in (-1, 0, 1) if (dx, dy) != (0, 0)]
SUM_START = (-1, 4, 7, 12)
SUM_MASKED = ((0, 1), (3, 4), (0, 1), (3, 4))


def iota(shape, dim):
    return lax.broadcasted_iota(jnp.int32, shape, dim)


def dot(a, b):
    return lax.dot_general(a, b, (((1,), (0,)), ((), ())), precision=HIGHEST, preferred_element_type=F32)


def dot_nt(a, b):
    return lax.dot_general(a, b, (((1,), (1,)), ((), ())), precision=HIGHEST, preferred_element_type=F32)


def kernel(n_x, n_y, ft_in, pt_in, sp_in, ow_in, pro, rows,
           ft, pt, sp, ow, own, rxl, rxh, ypl, yph, ryl, ryh, pd, rp, pe, ex, yz, fe, cf, mk, ba, bb, ap, wm, acc, xs, ct, pp, orow,
           snd, rcv, in_sem, x_send, x_recv, y_send, y_recv, p_send, p_recv, e_send, e_recv):
    gx = lax.axis_index("gx")
    gy = lax.axis_index("gy")
    peer = lambda dx, dy: (lax.rem(gx + (dx + n_x), n_x), lax.rem(gy + (dy + n_y), n_y))

    barrier = pltpu.get_barrier_semaphore()
    far = [j for j in range(1, n_y) if j not in (1, n_y - 1)]

    def inside(dx, dy):
        fits = None
        for d, at, count in ((dx, gx, n_x), (dy, gy, n_y)):
            if d:
                part = at > 0 if d < 0 else at < count - 1
                fits = part if fits is None else fits & part
        return fits

    for dx, dy in AROUND:
        def greet(dx=dx, dy=dy):
            pl.semaphore_signal(barrier, inc=1, device_id=peer(dx, dy), device_id_type=MESH)

        if dx == 0:
            greet()
        else:
            pl.when(inside(dx, dy))(greet)
    for j in far:
        pl.semaphore_signal(barrier, inc=1, device_id=peer(0, j), device_id_type=MESH)

    loads = [
        pltpu.make_async_copy(src, dst, in_sem.at[i])
        for i, (src, dst) in enumerate(((ft_in, ft), (pt_in, pt), (sp_in, sp), (ow_in, ow)))
    ]
    for copy in loads:
        copy.start()

    zero8 = jnp.zeros((8, 128), F32)

    def clear(x, carry):
        for s in range(8):
            for b in (ba, bb):
                b[s, x, 0:8, :] = zero8
                b[s, x, 32:40, :] = zero8
        for k in range(4):
            fe[k, x, 0:8, :] = zero8
        return carry

    lax.fori_loop(0, E, clear, 0)
    for copy in loads:
        copy.wait()

    pd[...] = jnp.zeros((8, 128), F32)
    for bx in range(2):
        total = None
        for k in range(6):
            place = (iota((16, 128), 1) == iota((16, 128), 0) + 16 * k).astype(F32)
            term = dot(sp[k, bx].astype(F32), place)
            total = term if total is None else total + term
        pd[2 * bx:2 * bx + 2, :] = total

    x_last = gx == n_x - 1
    y_last = gy == n_y - 1
    row16 = iota((16, 128), 0)
    lane16 = iota((16, 128), 1)
    keep_y = jnp.where((row16 == 15) & y_last, 0.0, 1.0)
    keep_z = jnp.where(lane16 == 127, 0.0, 1.0)

    def stage(x, carry):
        keep_x = jnp.where((x == 15) & x_last, 0.0, 1.0)
        p = pt[x]
        px = (p >= 9).astype(jnp.int32) + (p >= 18).astype(jnp.int32)
        q = p - 9 * px
        py = (q >= 3).astype(jnp.int32) + (q >= 6).astype(jnp.int32)
        pz = q - 3 * py
        bx = ((x >> 3) + px + 1) & 1
        by = ((row16 >> 3) + py + 1) & 1
        bz = ((lane16 >> 3) + pz + 1) & 1
        code = (4 * bx + 2 * by + bz).astype(F32)
        values = {FX: ft[0, x] * keep_x, FY: ft[1, x] * keep_y, FZ: ft[2, x] * keep_z, CODE: code}
        for k in range(4):
            own[x * 4 + k] = values[k]
            fe[k, x + 4, 12:28, :] = values[k]
            start = pl.multiple_of(x * 16, 8) + 4 * k
            ypl[pl.ds(start, 4), :] = values[k][0:4]
            yph[pl.ds(start, 4), :] = values[k][12:16]
        return carry

    lax.fori_loop(0, 16, stage, 0)
    sides_x = 2 - (gx == 0).astype(jnp.int32) - x_last.astype(jnp.int32)
    sides_y = 2 - (gy == 0).astype(jnp.int32) - y_last.astype(jnp.int32)
    pl.semaphore_wait(barrier, 2 + len(far) + sides_x * (1 + sides_y))

    def remote(src, dst, send, recv, dx, dy):
        return pltpu.make_async_remote_copy(src_ref=src, dst_ref=dst, send_sem=send, recv_sem=recv,
                                            device_id=peer(dx, dy), device_id_type=MESH)

    def between(act, copies, sign=1):
        for (dx, dy), copy in copies:
            pl.when(inside(sign * dx, sign * dy))(functools.partial(act, copy))

    def start(copies):
        between(lambda copy: copy.start(), copies)

    def arrive(copies):
        between(lambda copy: copy.wait_recv(), copies, -1)

    def leave(copies):
        between(lambda copy: copy.wait_send(), copies)

    def link(src, dst, send, recv, dx, dy):
        return (dx, dy), remote(src, dst, send, recv, dx, dy)

    pad_copies = [
        link(pd, rp.at[pl.ds(8 * d, 8)], p_send.at[d], p_recv.at[d], dx, dy) for d, (dx, dy) in enumerate(AROUND)
    ]
    y_copies = [
        link(yph, ryl.at[pl.ds(64, 256)], y_send.at[0], y_recv.at[0], 0, 1),
        link(ypl, ryh.at[pl.ds(64, 256)], y_send.at[1], y_recv.at[1], 0, -1),
    ]
    near_copies = [
        link(own.at[pl.ds(56, 8)], rxl.at[pl.ds(6, 8)], x_send.at[0], x_recv.at[0], 1, 0),
        link(own.at[pl.ds(0, 8)], rxh.at[pl.ds(0, 8)], x_send.at[1], x_recv.at[1], -1, 0),
    ]
    deep_copies = [
        link(own.at[pl.ds(50, 6)], rxl.at[pl.ds(0, 6)], x_send.at[2], x_recv.at[2], 1, 0),
        link(own.at[pl.ds(8, 4)], rxh.at[pl.ds(8, 4)], x_send.at[3], x_recv.at[3], -1, 0),
        link(own.at[pl.ds(15, 1)], rxh.at[pl.ds(12, 1)], x_send.at[4], x_recv.at[4], -1, 0),
    ]
    near_corners, deep_corners = [], []
    for corners, from_low, to_low, from_high, to_high in (
            (near_corners, 224, 32, 0, 320), (deep_corners, 192, 0, 32, 352)):
        for src, dst, dy in ((yph, ryl, 1), (ypl, ryh, -1)):
            for dx, a, b in ((1, from_low, to_low), (-1, from_high, to_high)):
                at = 2 + len(near_corners) + len(deep_corners)
                corners.append(link(src.at[pl.ds(a, 32)], dst.at[pl.ds(b, 32)], y_send.at[at], y_recv.at[at], dx, dy))
    start(near_copies)
    start(pad_copies)
    start(y_copies)
    start(near_corners)
    start(deep_copies)
    start(deep_corners)
    near_copies += near_corners
    deep_copies += deep_corners

    def beyond(ref, layers_of_x, code):
        for x in layers_of_x:
            ref[16 * x:16 * x + 16, :] = jnp.ones((16, 128), F32)
            ref[16 * x + 4 * CODE:16 * x + 4 * CODE + 4, :] = jnp.full((4, 128), code, F32)

    def closed_west():
        for r in (ryl, ryh):
            r[48 + 4 * FX:52 + 4 * FX, :] = jnp.zeros((4, 128), F32)

    @pl.when(gx == 0)
    def _():
        for i in range(14):
            k = (50 + i) % 4
            rxl[i] = jnp.full((16, 128), 6.0 if k == CODE else 0.0 if (k, i) == (FX, 12) else 1.0, F32)
        beyond(ryl, range(4), 6.0)
        beyond(ryh, range(4), 6.0)
        closed_west()

    @pl.when(x_last)
    def _():
        rxh[...] = jnp.ones_like(rxh)
        beyond(ryl, range(20, 24), 1.0)
        beyond(ryh, range(20, 24), 1.0)

    @pl.when(gy == 0)
    def _():
        beyond(ryl, range(E), 6.0)
        for x in range(E):
            ryl[16 * x + 4 * FY + 3:16 * x + 4 * FY + 4, :] = jnp.zeros((1, 128), F32)
        pl.when(gx == 0)(closed_west)

    @pl.when(y_last)
    def _():
        beyond(ryh, range(E), 1.0)
        pl.when(gx == 0)(closed_west)

    orow[...] = jnp.full((8, 128), -1.0, F32)
    orow[0:1, 0:64] = ow[...].astype(F32)
    owner = jnp.broadcast_to(orow[0:1, :], (128, 128))
    earlier = (owner == owner.T) & (iota((128, 128), 0) < iota((128, 128), 1))
    rank = jnp.sum(earlier.astype(F32), axis=0, keepdims=True)
    target = orow[0:1, :] * 8.0 + rank
    row_f = iota((128, 128), 0).astype(F32)
    for b in range(4):
        shifted = jnp.broadcast_to(target, (8, 128))
        if b:
            shifted = pltpu.roll(shifted, 128 - 16 * b, 1)
        pp[b] = ((row_f == shifted[0:1]) & (iota((128, 128), 1) < 16)).astype(F32)

    c = iota((128, 256), 1)
    up_z, b_x, up_x, b_y, up_y = c >> 7, (c >> 6) & 1, (c >> 5) & 1, (c >> 4) & 1, (c >> 3) & 1
    s_x, s_y, s_z = (c >> 2) & 1, (c >> 1) & 1, c & 1
    o_x = jnp.where(s_x == b_x, 1, 2 * up_x)
    o_y = jnp.where(s_y == b_y, 1, 2 * up_y)
    o_z = jnp.where(s_z == 0, 1, 2 * up_z)
    ct[...] = (iota((128, 256), 0) == (b_x * 2 + b_y) * 32 + 9 * o_x + 3 * o_y + o_z).astype(F32)

    arrive(pad_copies)
    low = {-1: 0, 0: 1, 1: 3}
    for dx, dy in AROUND + [(0, 0)]:
        sx, sy = -dx, -dy
        base = 0 if (dx, dy) == (0, 0) else 8 * AROUND.index((dx, dy))
        src = pd if (dx, dy) == (0, 0) else rp
        for i in ((1,) if sx < 0 else (0,) if sx > 0 else (0, 1)):
            for j in ((1,) if sy < 0 else (0,) if sy > 0 else (0, 1)):
                bi = low[sx] + (i if sx == 0 else 0)
                bj = low[sy] + (j if sy == 0 else 0)
                pe[4 * bi + bj:4 * bi + bj + 1, :] = src[base + 2 * i + j:base + 2 * i + j + 1, :]
    block_row = iota((16, 128), 0)
    outside = ((((block_row >> 2) == 0) & (gx == 0)) | (((block_row >> 2) == 3) & x_last)
               | (((block_row & 3) == 0) & (gy == 0)) | (((block_row & 3) == 3) & y_last))
    pads = jnp.where(outside, 0.0, pe[...])
    r_in = iota((128, 128), 0)
    tile_z = (iota((128, 128), 1) + 4) >> 3
    for sz in range(2):
        upper = (tile_z & 1) == sz
        bz = jnp.where(upper, tile_z, tile_z - 1)
        fits = (bz >= 0) & (bz < 16)
        for k in range(5):
            lanes = bz + 16 * k if k < 4 else bz + jnp.where(upper, 64, 80)
            ex[sz * 5 + k] = dot(pads, (fits & (r_in == lanes)).astype(F32))

    row8 = iota((8, 128), 0).astype(F32)
    lane8 = iota((8, 128), 1)
    i_z = ((lane8 + 4) & 7).astype(F32)
    up8 = ((lane8 + 4) >> 3) & 1
    for s in range(8):
        sx, sy, sz = s >> 2, (s >> 1) & 1, s & 1
        for g in range(3):
            bx = g if g % 2 == sx else g - 1
            for t in range(3):
                by = t if t % 2 == sy else t - 1
                r = (bx + 1) * 4 + by + 1
                reach_z = ex[sz * 5 + 4, r:r + 1, :]
                ok_z = jnp.where(up8 == sz, i_z + reach_z, 7.0 - i_z + reach_z) >= 4.0
                if by == t:
                    ok_y = row8 + ex[sz * 5 + 2, r:r + 1, :] >= 4.0
                else:
                    ok_y = row8 <= 3.0 + ex[sz * 5 + 3, r:r + 1, :]
                yz[s, g, 8 * t:8 * t + 8, :] = (ok_z & ok_y).astype(F32)

    def masks(i, carry):
        at = i.astype(F32)
        for s in range(8):
            sx, sy, sz = s >> 2, (s >> 1) & 1, s & 1
            for g in range(3):
                bx = g if g % 2 == sx else g - 1
                for t in range(3):
                    by = t if t % 2 == sy else t - 1
                    r = (bx + 1) * 4 + by + 1
                    if bx == g:
                        ok_x = ex[sz * 5, r:r + 1, :] >= 4.0 - at
                    else:
                        ok_x = ex[sz * 5 + 1, r:r + 1, :] >= at - 3.0
                    mk[s, 8 * g + i, 8 * t:8 * t + 8, :] = jnp.where(ok_x, yz[s, g, 8 * t:8 * t + 8, :], 0.0)
        return carry

    lax.fori_loop(0, 8, masks, 0, unroll=4)

    arrive(y_copies)

    def unpack(x):
        for k in range(4):
            start = 16 * x + 4 * k
            if not isinstance(x, int):
                start = pl.multiple_of(x * 16, 8) + 4 * k
            fe[k, x, 8:12, :] = ryl[pl.ds(start, 4), :]
            fe[k, x, 28:32, :] = ryh[pl.ds(start, 4), :]

    def first(x):
        for t in range(3):
            code = fe[CODE, x, 8 + 8 * t:16 + 8 * t, :]
            for s in range(8):
                ba[s, x, 8 + 8 * t:16 + 8 * t, :] = (code == float(s)).astype(F32)

    def coefficients(x):
        for t in range(3):
            a, b = 8 + 8 * t, 16 + 8 * t
            east, west = fe[FX, x, a:b, :], fe[FX, x - 1, a:b, :]
            north, south = fe[FY, x, a:b, :], fe[FY, x, a - 1:b - 1, :]
            top = fe[FZ, x, a:b, :]
            bottom = pltpu.roll(top, 1, 1)
            diagonal = west + east + south + north + bottom + top
            inverse = 1.0 / diagonal
            for i, face in enumerate((east, west, north, south, top, bottom)):
                cf[i, x, 8 * t:8 * t + 8, :] = face * inverse
            cf[6, x, 8 * t:8 * t + 8, :] = diagonal

    def around(src, s, x, t, faces):
        east, west, north, south, top, bottom = faces
        a, b = 8 + 8 * t, 16 + 8 * t
        centre = src[s, x, a:b, :]
        total = (east * src[s, x + 1, a:b, :] + west * src[s, x - 1, a:b, :]
                 + north * src[s, x, a + 1:b + 1, :] + south * src[s, x, a - 1:b - 1, :]
                 + top * pltpu.roll(centre, 127, 1) + bottom * pltpu.roll(centre, 1, 1))
        return centre, total

    def smooth(src, dst, x):
        for t in range(3):
            faces = [cf[i, x, 8 * t:8 * t + 8, :] for i in range(6)]
            updated = []
            for s in range(8):
                centre, total = around(src, s, x, t, faces)
                updated.append(mk[s, x, 8 * t:8 * t + 8, :] * (0.5 * centre + total))
            whole = ((updated[0] + updated[1]) + (updated[2] + updated[3])) + (
                (updated[4] + updated[5]) + (updated[6] + updated[7]))
            scale = 1.0 / jnp.where(whole > 0.0, whole, 1.0)
            for s in range(8):
                dst[s, x, 8 + 8 * t:16 + 8 * t, :] = updated[s] * scale

    def apply(x):
        for t in range(3):
            faces = [cf[i, x, 8 * t:8 * t + 8, :] for i in range(6)]
            diagonal = cf[6, x, 8 * t:8 * t + 8, :]
            for s in range(8):
                centre, total = around(ba, s, x, t, faces)
                ap[s, x, 8 * t:8 * t + 8, :] = diagonal * (centre - total)

    def weigh(a):
        for i in range(5):
            x = SUM_START[a] + 4 + i
            for t in range(3):
                code = fe[CODE, x, 8 + 8 * t:16 + 8 * t, :].astype(jnp.int32)
                in_x = (((code >> 2) & 1) == a // 2).astype(F32)
                odd_y = ((code >> 1) & 1).astype(F32)
                odd_z = (code & 1).astype(F32)
                in_y = 1.0 - odd_y if t == 0 else odd_y
                wm[a * 5 + i, 0, 8 * t:8 * t + 8, :] = in_x
                wm[a * 5 + i, 1, 8 * t:8 * t + 8, :] = in_x * odd_z
                wm[a * 5 + i, 2, 8 * t:8 * t + 8, :] = in_x * in_y
                wm[a * 5 + i, 3, 8 * t:8 * t + 8, :] = in_x * in_y * odd_z

    def sums(a, s):
        for t in range(3):
            parts = [None] * 4
            for i in range(5):
                value = ap[s, SUM_START[a] + 4 + i, 8 * t:8 * t + 8, :]
                for m in range(4) if t == 1 else (2, 3):
                    if m == 0 and i not in SUM_MASKED[a]:
                        term = value
                    else:
                        term = value * wm[a * 5 + i, m, 8 * t:8 * t + 8, :]
                    parts[m] = term if parts[m] is None else parts[m] + term
            for m in range(4) if t == 1 else (2, 3):
                place = a * 8 + (m - 2 if t == 0 else m + 2 if t == 1 else m + 4)
                acc[pl.ds(pl.multiple_of((place * 8 + s) * 8, 8), 8), :] = parts[m]

    def over_rows(a):
        r = []
        for place in range(a * 8, a * 8 + 8):
            total = acc[pl.ds(place * 64, 8, stride=8), :]
            for y in range(1, 8):
                total = total + acc[pl.ds(place * 64 + y, 8, stride=8), :]
            r.append(total)
        r[2], r[3] = r[2] - r[4], r[3] - r[5]
        for b in range(4):
            for m in range(2):
                start = m * 128 + (a * 4 + b) * 8
                xs[start:start + 8, :] = r[2 * b + m]

    def layers(step, start, stop, unroll):
        def body(x, carry):
            step(x)
            return carry

        lax.fori_loop(start, stop, body, 0, unroll=unroll)

    def both(step, start, other, count, unroll):
        def body(i, carry):
            step(start + i)
            step(other + i)
            return carry

        lax.fori_loop(0, count, body, 0, unroll=unroll)

    def give(x):
        for s in range(8):
            pro[s, x] = ba[s, x + 4, 12:28, :]

    once = functools.partial(smooth, ba, bb)
    twice = functools.partial(smooth, bb, ba)

    layers(unpack, 4, 20, 8)
    layers(first, 4, 20, 8)
    layers(coefficients, 5, 20, 5)
    layers(once, 5, 19, 7)
    layers(twice, 6, 18, 6)
    layers(give, 2, 14, 4)
    layers(apply, 7, 17, 5)
    weigh(1)
    weigh(2)
    layers(functools.partial(sums, 1), 0, 8, 4)
    layers(functools.partial(sums, 2), 0, 8, 4)

    arrive(near_copies)
    for i in range(8):
        fe[i % 4, 2 + i // 4, 12:28, :] = rxl[6 + i]
        fe[i % 4, 20 + i // 4, 12:28, :] = rxh[i]
    for x in (2, 3, 20, 21):
        unpack(x)
    both(first, 2, 20, 2, 2)
    both(coefficients, 3, 20, 2, 2)
    both(once, 3, 19, 2, 2)
    both(twice, 4, 18, 2, 2)
    both(give, 0, 14, 2, 2)
    both(apply, 5, 17, 2, 2)
    weigh(0)
    weigh(3)

    arrive(deep_copies)
    for i in range(6):
        flat = 50 + i
        fe[flat % 4, flat // 4 - 12, 12:28, :] = rxl[i]
    for i in range(4):
        fe[i, 22, 12:28, :] = rxh[8 + i]
    fe[CODE, 23, 12:28, :] = rxh[12]
    for x in (0, 1, 22, 23):
        unpack(x)
    both(first, 0, 22, 2, 2)
    both(coefficients, 1, 22, 1, 1)
    coefficients(2)
    both(once, 1, 21, 2, 2)
    both(twice, 2, 20, 2, 2)
    both(apply, 3, 19, 2, 2)
    layers(functools.partial(sums, 0), 0, 8, 4)
    layers(functools.partial(sums, 3), 0, 8, 4)
    for a in range(4):
        over_rows(a)

    lane_tile = (iota((128, 128), 0) + 4) >> 3
    col = iota((128, 128), 1)
    even = (col & 1) == 0
    even_row = (iota((128, 128), 0) & 1) == 0
    halves = []
    for up in range(2):
        gather = ((lane_tile == col + up) & (col < 16)).astype(F32)
        z = dot(xs[...], gather)
        v = jnp.where(even, z[0:128] - z[128:256], z[128:256])
        other = jnp.where(even_row, pltpu.roll(v, 127, 0), pltpu.roll(v, 1, 0))
        halves.append(jnp.where(even, v, other))
    entries = dot(ct[:, 0:128], halves[0]) + dot(ct[:, 128:256], halves[1])
    routed = dot_nt(pp[0], entries[0:32])
    for b in range(1, 4):
        routed = routed + dot_nt(pp[b], entries[32 * b:32 * b + 32])
    snd[:, 0:32] = routed
    snd[:, 32:128] = jnp.zeros((128, 96), F32)

    mine = pl.multiple_of(gy * 8, 8)
    sent = []
    for j in range(1, n_y):
        there = lax.rem(gy + j, n_y)
        copy = remote(snd.at[pl.ds(pl.multiple_of(there * 8, 8), 8)], rcv.at[pl.ds(mine, 8)],
                      e_send.at[j], e_recv.at[j], 0, j)
        copy.start()
        sent.append(copy)
    rcv[pl.ds(mine, 8), :] = snd[pl.ds(mine, 8), :]
    for copy in sent:
        copy.wait_recv()
    rows[:, 0, :] = rcv[...].T[0:27, :]
    leave(pad_copies + y_copies + near_copies + deep_copies)
    for copy in sent:
        copy.wait_send()


def writer(pro, rows, pro_out, rows_out, sem):
    copies = [pltpu.make_async_copy(pro, pro_out, sem.at[0]), pltpu.make_async_copy(rows, rows_out, sem.at[1])]
    for copy in copies:
        copy.start()
    for copy in copies:
        copy.wait()


def solution(mesh):
    n_x, n_y = mesh.shape["gx"], mesh.shape["gy"]
    hbm = pl.BlockSpec(memory_space=pltpu.HBM)
    vmem = pl.BlockSpec(memory_space=pltpu.VMEM)
    dma = pltpu.SemaphoreType.DMA

    def on_device(face_trans, partition, support_pad, owners):
        prolongation, rows = pl.pallas_call(
            functools.partial(kernel, n_x, n_y),
            out_shape=(
                pltpu.VMEM((8, 16, 16, 128), F32),
                pltpu.VMEM((27, 1, 128), F32),
            ),
            in_specs=[hbm] * 4,
            out_specs=(vmem, vmem),
            scratch_shapes=[
                pltpu.VMEM((3, 16, 16, 128), F32),
                pltpu.VMEM((16, 16, 128), jnp.int32),
                pltpu.VMEM((6, 2, 2, 16), jnp.int32),
                pltpu.VMEM((1, 64), jnp.int32),
                pltpu.VMEM((64, 16, 128), F32),
                pltpu.VMEM((14, 16, 128), F32),
                pltpu.VMEM((13, 16, 128), F32),
                pltpu.VMEM((256, 128), F32),
                pltpu.VMEM((256, 128), F32),
                pltpu.VMEM((384, 128), F32),
                pltpu.VMEM((384, 128), F32),
                pltpu.VMEM((8, 128), F32),
                pltpu.VMEM((64, 128), F32),
                pltpu.VMEM((16, 128), F32),
                pltpu.VMEM((10, 16, 128), F32),
                pltpu.VMEM((8, 3, E, 128), F32),
                pltpu.VMEM((4, E, 40, 128), F32),
                pltpu.VMEM((7, E, E, 128), F32),
                pltpu.VMEM((8, E, E, 128), F32),
                pltpu.VMEM((8, E, 40, 128), F32),
                pltpu.VMEM((8, E, 40, 128), F32),
                pltpu.VMEM((8, E, E, 128), F32),
                pltpu.VMEM((20, 4, E, 128), F32),
                pltpu.VMEM((2048, 128), F32),
                pltpu.VMEM((256, 128), F32),
                pltpu.VMEM((128, 256), F32),
                pltpu.VMEM((4, 128, 128), F32),
                pltpu.VMEM((8, 128), F32),
                pltpu.VMEM((128, 128), F32),
                pltpu.VMEM((8 * n_y, 128), F32),
                dma((4,)), dma((5,)), dma((5,)), dma((10,)), dma((10,)), dma((8,)), dma((8,)), dma((n_y,)), dma((n_y,)),
            ],
            compiler_params=pltpu.CompilerParams(
                collective_id=0, has_side_effects=True, vmem_limit_bytes=48 * 2**20
            ),
        )(*(pltpu.with_memory_space_constraint(a, pltpu.HBM)
            for a in (face_trans, partition, support_pad, owners.reshape(1, 64))))
        prolongation, rows = pl.pallas_call(
            writer,
            out_shape=(
                jax.ShapeDtypeStruct((8, 16, 16, 128), F32),
                jax.ShapeDtypeStruct((27, 1, 128), F32),
            ),
            in_specs=[vmem] * 2,
            out_specs=(hbm, hbm),
            scratch_shapes=[dma((2,))],
        )(*(pltpu.with_memory_space_constraint(a, pltpu.VMEM) for a in (prolongation, rows)))
        return prolongation, rows.reshape(1, 1, 27, 128)

    placed = (
        P(None, "gx", "gy", None),
        P("gx", "gy", None),
        P(None, "gx", "gy", None),
        P("gx", "gy", None, None),
    )
    return jax.shard_map(
        on_device,
        mesh=mesh,
        in_specs=placed,
        out_specs=(P(None, "gx", "gy", None), P("gx", "gy", None, None)),
        check_vma=False,
    )
```

```python
import functools

import jax
import jax.numpy as jnp
from jax import lax
from jax.experimental import pallas as pl
from jax.experimental.pallas import tpu as pltpu
from jax.sharding import PartitionSpec as P

MESH = pl.DeviceIdType.MESH
F32 = jnp.float32

E = 24
FY, FZ, FX, CODE = range(4)
AROUND = [(dx, dy) for dx in (-1, 0, 1) for dy in (-1, 0, 1) if (dx, dy) != (0, 0)]
CORNERS = [(dx, dy) for dx in (1, -1) for dy in (1, -1)]
SUM_START = (-1, 4, 7, 12)
SUM_MASKED = ((0, 1), (3, 4), (0, 1), (3, 4))


def iota(shape, dim):
    return lax.broadcasted_iota(jnp.int32, shape, dim)


def parts(a):
    high = a.astype(jnp.bfloat16)
    rest = a - high.astype(F32)
    middle = rest.astype(jnp.bfloat16)
    return high, middle, (rest - middle.astype(F32)).astype(jnp.bfloat16)


def dot(a, b, dims=(((1,), (0,)), ((), ()))):
    total = None
    exact = a.astype(jnp.bfloat16)
    for part in parts(b):
        term = lax.dot_general(exact, part, dims, preferred_element_type=F32)
        total = term if total is None else total + term
    return total


def dot_left(a, b):
    total = None
    exact = b.astype(jnp.bfloat16)
    for part in parts(a):
        term = lax.dot_general(part, exact, (((1,), (0,)), ((), ())), preferred_element_type=F32)
        total = term if total is None else total + term
    return total


def dot_nt(a, b):
    return dot(a, b, (((1,), (1,)), ((), ())))


def kernel(n_x, n_y, ft_in, pt_in, sp_in, ow_in, pro, rows,
           ft, pt, sp, ow, own, rxl, rxh, ypl, yph, ryl, ryh, cpk, crx, pd, rp, pe, ex, yz, fe, cf, mk, ba, bb, ap, wm, acc, xs, ct, pp, orow,
           snd, rcv, in_sem, x_send, x_recv, y_send, y_recv, p_send, p_recv, e_send, e_recv):
    gx = lax.axis_index("gx")
    gy = lax.axis_index("gy")
    peer = lambda dx, dy: (lax.rem(gx + (dx + n_x), n_x), lax.rem(gy + (dy + n_y), n_y))

    barrier = pltpu.get_barrier_semaphore()
    far = [j for j in range(1, n_y) if j not in (1, n_y - 1)]

    def inside(dx, dy):
        fits = None
        for d, at, count in ((dx, gx, n_x), (dy, gy, n_y)):
            if d:
                part = at > 0 if d < 0 else at < count - 1
                fits = part if fits is None else fits & part
        return fits

    for dx, dy in AROUND:
        def greet(dx=dx, dy=dy):
            pl.semaphore_signal(barrier, inc=1, device_id=peer(dx, dy), device_id_type=MESH)

        if dx == 0:
            greet()
        else:
            pl.when(inside(dx, dy))(greet)
    for j in far:
        pl.semaphore_signal(barrier, inc=1, device_id=peer(0, j), device_id_type=MESH)

    loads = [
        pltpu.make_async_copy(src, dst, in_sem.at[i])
        for i, (src, dst) in enumerate(((ft_in, ft), (pt_in, pt), (sp_in, sp), (ow_in, ow)))
    ]
    for copy in loads:
        copy.start()

    zero8 = jnp.zeros((8, 128), F32)

    def clear(x, carry):
        for s in range(8):
            for b in (ba, bb):
                b[s, x, 0:8, :] = zero8
                b[s, x, 32:40, :] = zero8
        for k in range(4):
            fe[k, x, 0:8, :] = zero8
        return carry

    lax.fori_loop(0, E, clear, 0)
    for c in range(4):
        cpk[c, 8:16, :] = zero8
    for x in (0, 1, 22, 23):
        for k in range(4):
            fe[k, x, 8:16, :] = jnp.ones((8, 128), F32)
            fe[k, x, 24:32, :] = jnp.ones((8, 128), F32)
    for copy in loads:
        copy.wait()

    pd[...] = jnp.zeros((8, 128), F32)
    for bx in range(2):
        total = None
        for k in range(6):
            place = (iota((16, 128), 1) == iota((16, 128), 0) + 16 * k).astype(F32)
            term = dot(sp[k, bx].astype(F32), place)
            total = term if total is None else total + term
        pd[2 * bx:2 * bx + 2, :] = total

    x_last = gx == n_x - 1
    y_last = gy == n_y - 1
    row16 = iota((16, 128), 0)
    lane16 = iota((16, 128), 1)
    keep_y = jnp.where((row16 == 15) & y_last, 0.0, 1.0)
    keep_z = jnp.where(lane16 == 127, 0.0, 1.0)

    def stage(x, carry):
        keep_x = jnp.where((x == 15) & x_last, 0.0, 1.0)
        p = pt[x]
        px = (p >= 9).astype(jnp.int32) + (p >= 18).astype(jnp.int32)
        q = p - 9 * px
        py = (q >= 3).astype(jnp.int32) + (q >= 6).astype(jnp.int32)
        pz = q - 3 * py
        bx = ((x >> 3) + px + 1) & 1
        by = ((row16 >> 3) + py + 1) & 1
        bz = ((lane16 >> 3) + pz + 1) & 1
        code = (4 * bx + 2 * by + bz).astype(F32)
        values = {FX: ft[0, x] * keep_x, FY: ft[1, x] * keep_y, FZ: ft[2, x] * keep_z, CODE: code}
        for k in range(4):
            own[x * 4 + k] = values[k]
            fe[k, x + 4, 12:28, :] = values[k]
            start = pl.multiple_of(x * 16, 8) + 4 * k
            ypl[pl.ds(start, 4), :] = values[k][0:4]
            yph[pl.ds(start, 4), :] = values[k][12:16]
        return carry

    lax.fori_loop(0, 16, stage, 0)
    for c, (dx, dy) in enumerate(CORNERS):
        a, b = (13, 12) if dx > 0 else (2, 3)
        y, edge = (14, 15) if dy > 0 else (0, 0)
        for k in range(4):
            cpk[c, 2 * k:2 * k + 2, :] = own[a * 4 + k, y:y + 2, :]
        cpk[c, 8:9, :] = own[b * 4 + FX, edge:edge + 1, :]
        cpk[c, 9:10, :] = own[b * 4 + CODE, edge:edge + 1, :]
    sides_x = 2 - (gx == 0).astype(jnp.int32) - x_last.astype(jnp.int32)
    sides_y = 2 - (gy == 0).astype(jnp.int32) - y_last.astype(jnp.int32)
    pl.semaphore_wait(barrier, 2 + len(far) + sides_x * (1 + sides_y))

    def remote(src, dst, send, recv, dx, dy):
        return pltpu.make_async_remote_copy(src_ref=src, dst_ref=dst, send_sem=send, recv_sem=recv,
                                            device_id=peer(dx, dy), device_id_type=MESH)

    def between(act, copies, sign=1):
        for (dx, dy), copy in copies:
            pl.when(inside(sign * dx, sign * dy))(functools.partial(act, copy))

    def start(copies):
        between(lambda copy: copy.start(), copies)

    def arrive(copies):
        between(lambda copy: copy.wait_recv(), copies, -1)

    def leave(copies):
        between(lambda copy: copy.wait_send(), copies)

    def link(src, dst, send, recv, dx, dy):
        return (dx, dy), remote(src, dst, send, recv, dx, dy)

    pad_copies = [
        link(pd, rp.at[pl.ds(8 * d, 8)], p_send.at[d], p_recv.at[d], dx, dy) for d, (dx, dy) in enumerate(AROUND)
    ]
    y_copies = [
        link(yph, ryl.at[pl.ds(64, 256)], y_send.at[0], y_recv.at[0], 0, 1),
        link(ypl, ryh.at[pl.ds(64, 256)], y_send.at[1], y_recv.at[1], 0, -1),
    ]
    near_copies = [
        link(own.at[pl.ds(56, 8)], rxl.at[pl.ds(6, 8)], x_send.at[0], x_recv.at[0], 1, 0),
        link(own.at[pl.ds(0, 8)], rxh.at[pl.ds(0, 8)], x_send.at[1], x_recv.at[1], -1, 0),
    ]
    deep_copies = [
        link(own.at[pl.ds(50, 6)], rxl.at[pl.ds(0, 6)], x_send.at[2], x_recv.at[2], 1, 0),
        link(own.at[pl.ds(8, 4)], rxh.at[pl.ds(8, 4)], x_send.at[3], x_recv.at[3], -1, 0),
        link(own.at[pl.ds(15, 1)], rxh.at[pl.ds(12, 1)], x_send.at[4], x_recv.at[4], -1, 0),
    ]
    near_corners, deep_corners = [], []
    for c, (dx, dy) in enumerate(CORNERS):
        src, dst = (yph, ryl) if dy > 0 else (ypl, ryh)
        a, b = (224, 32) if dx > 0 else (0, 320)
        near_corners.append(
            link(src.at[pl.ds(a, 32)], dst.at[pl.ds(b, 32)], y_send.at[2 + c], y_recv.at[2 + c], dx, dy))
        deep_corners.append(link(cpk.at[c], crx.at[c], y_send.at[6 + c], y_recv.at[6 + c], dx, dy))
    start(near_copies)
    start(pad_copies)
    start(y_copies)
    start(near_corners)
    start(deep_copies)
    start(deep_corners)

    for (dx, dy), c in zip(CORNERS, range(4)):
        def fill(c=c, dy=dy):
            crx[c] = jnp.ones((16, 128), F32)
            if dy > 0:
                crx[c, 2 * FY + 1:2 * FY + 2, :] = jnp.zeros((1, 128), F32)

        pl.when(jnp.logical_not(inside(-dx, -dy)))(fill)

    near_copies += near_corners
    deep_copies += deep_corners

    def beyond(ref, layers_of_x, code):
        for x in layers_of_x:
            ref[16 * x:16 * x + 16, :] = jnp.ones((16, 128), F32)
            ref[16 * x + 4 * CODE:16 * x + 4 * CODE + 4, :] = jnp.full((4, 128), code, F32)

    def closed_west():
        for r in (ryl, ryh):
            r[48 + 4 * FX:52 + 4 * FX, :] = jnp.zeros((4, 128), F32)

    @pl.when(gx == 0)
    def _():
        for i in range(14):
            k = (50 + i) % 4
            rxl[i] = jnp.full((16, 128), 6.0 if k == CODE else 0.0 if (k, i) == (FX, 12) else 1.0, F32)
        beyond(ryl, range(4), 6.0)
        beyond(ryh, range(4), 6.0)
        closed_west()

    @pl.when(x_last)
    def _():
        rxh[...] = jnp.ones_like(rxh)
        beyond(ryl, range(20, 24), 1.0)
        beyond(ryh, range(20, 24), 1.0)

    @pl.when(gy == 0)
    def _():
        beyond(ryl, range(E), 6.0)
        for x in range(E):
            ryl[16 * x + 4 * FY + 3:16 * x + 4 * FY + 4, :] = jnp.zeros((1, 128), F32)
        pl.when(gx == 0)(closed_west)

    @pl.when(y_last)
    def _():
        beyond(ryh, range(E), 1.0)
        pl.when(gx == 0)(closed_west)

    orow[...] = jnp.full((8, 128), -1.0, F32)
    orow[0:1, 0:64] = ow[...].astype(F32)
    owner = jnp.broadcast_to(orow[0:1, :], (128, 128))
    earlier = (owner == owner.T) & (iota((128, 128), 0) < iota((128, 128), 1))
    rank = jnp.sum(earlier.astype(F32), axis=0, keepdims=True)
    target = orow[0:1, :] * 8.0 + rank
    row_f = iota((128, 128), 0).astype(F32)
    for b in range(4):
        shifted = jnp.broadcast_to(target, (8, 128))
        if b:
            shifted = pltpu.roll(shifted, 128 - 16 * b, 1)
        pp[b] = ((row_f == shifted[0:1]) & (iota((128, 128), 1) < 16)).astype(F32)

    c = iota((128, 256), 1)
    up_z, b_x, up_x, b_y, up_y = c >> 7, (c >> 6) & 1, (c >> 5) & 1, (c >> 4) & 1, (c >> 3) & 1
    s_x, s_y, s_z = (c >> 2) & 1, (c >> 1) & 1, c & 1
    o_x = jnp.where(s_x == b_x, 1, 2 * up_x)
    o_y = jnp.where(s_y == b_y, 1, 2 * up_y)
    o_z = jnp.where(s_z == 0, 1, 2 * up_z)
    ct[...] = (iota((128, 256), 0) == (b_x * 2 + b_y) * 32 + 9 * o_x + 3 * o_y + o_z).astype(F32)

    arrive(pad_copies)
    low = {-1: 0, 0: 1, 1: 3}
    for dx, dy in AROUND + [(0, 0)]:
        sx, sy = -dx, -dy
        base = 0 if (dx, dy) == (0, 0) else 8 * AROUND.index((dx, dy))
        src = pd if (dx, dy) == (0, 0) else rp
        for i in ((1,) if sx < 0 else (0,) if sx > 0 else (0, 1)):
            for j in ((1,) if sy < 0 else (0,) if sy > 0 else (0, 1)):
                bi = low[sx] + (i if sx == 0 else 0)
                bj = low[sy] + (j if sy == 0 else 0)
                pe[4 * bi + bj:4 * bi + bj + 1, :] = src[base + 2 * i + j:base + 2 * i + j + 1, :]
    block_row = iota((16, 128), 0)
    outside = ((((block_row >> 2) == 0) & (gx == 0)) | (((block_row >> 2) == 3) & x_last)
               | (((block_row & 3) == 0) & (gy == 0)) | (((block_row & 3) == 3) & y_last))
    pads = jnp.where(outside, 0.0, pe[...])
    r_in = iota((128, 128), 0)
    tile_z = (iota((128, 128), 1) + 4) >> 3
    for sz in range(2):
        upper = (tile_z & 1) == sz
        bz = jnp.where(upper, tile_z, tile_z - 1)
        fits = (bz >= 0) & (bz < 16)
        for k in range(5):
            lanes = bz + 16 * k if k < 4 else bz + jnp.where(upper, 64, 80)
            ex[sz * 5 + k] = dot(pads, (fits & (r_in == lanes)).astype(F32))

    row8 = iota((8, 128), 0).astype(F32)
    lane8 = iota((8, 128), 1)
    i_z = ((lane8 + 4) & 7).astype(F32)
    up8 = ((lane8 + 4) >> 3) & 1
    for s in range(8):
        sx, sy, sz = s >> 2, (s >> 1) & 1, s & 1
        for g in range(3):
            bx = g if g % 2 == sx else g - 1
            for t in range(3):
                by = t if t % 2 == sy else t - 1
                r = (bx + 1) * 4 + by + 1
                reach_z = ex[sz * 5 + 4, r:r + 1, :]
                ok_z = jnp.where(up8 == sz, i_z + reach_z, 7.0 - i_z + reach_z) >= 4.0
                if by == t:
                    ok_y = row8 + ex[sz * 5 + 2, r:r + 1, :] >= 4.0
                else:
                    ok_y = row8 <= 3.0 + ex[sz * 5 + 3, r:r + 1, :]
                yz[s, g, 8 * t:8 * t + 8, :] = (ok_z & ok_y).astype(F32)

    def masks(i, carry):
        at = i.astype(F32)
        for s in range(8):
            sx, sy, sz = s >> 2, (s >> 1) & 1, s & 1
            for g in range(3):
                bx = g if g % 2 == sx else g - 1
                for t in range(3):
                    by = t if t % 2 == sy else t - 1
                    r = (bx + 1) * 4 + by + 1
                    if bx == g:
                        ok_x = ex[sz * 5, r:r + 1, :] >= 4.0 - at
                    else:
                        ok_x = ex[sz * 5 + 1, r:r + 1, :] >= at - 3.0
                    mk[s, 8 * g + i, 8 * t:8 * t + 8, :] = jnp.where(ok_x, yz[s, g, 8 * t:8 * t + 8, :], 0.0)
        return carry

    lax.fori_loop(0, 8, masks, 0, unroll=4)

    arrive(y_copies)

    def unpack(x):
        for k in range(4):
            start = 16 * x + 4 * k
            if not isinstance(x, int):
                start = pl.multiple_of(x * 16, 8) + 4 * k
            fe[k, x, 8:12, :] = ryl[pl.ds(start, 4), :]
            fe[k, x, 28:32, :] = ryh[pl.ds(start, 4), :]

    def first(x):
        for t in range(3):
            code = fe[CODE, x, 8 + 8 * t:16 + 8 * t, :]
            for s in range(8):
                ba[s, x, 8 + 8 * t:16 + 8 * t, :] = (code == float(s)).astype(F32)

    def coefficients(x):
        for t in range(3):
            a, b = 8 + 8 * t, 16 + 8 * t
            east, west = fe[FX, x, a:b, :], fe[FX, x - 1, a:b, :]
            north, south = fe[FY, x, a:b, :], fe[FY, x, a - 1:b - 1, :]
            top = fe[FZ, x, a:b, :]
            bottom = pltpu.roll(top, 1, 1)
            diagonal = west + east + south + north + bottom + top
            inverse = 1.0 / diagonal
            for i, face in enumerate((east, west, north, south, top, bottom)):
                cf[i, x, 8 * t:8 * t + 8, :] = face * inverse
            cf[6, x, 8 * t:8 * t + 8, :] = diagonal

    def around(src, s, x, t, faces):
        east, west, north, south, top, bottom = faces
        a, b = 8 + 8 * t, 16 + 8 * t
        centre = src[s, x, a:b, :]
        total = (east * src[s, x + 1, a:b, :] + west * src[s, x - 1, a:b, :]
                 + north * src[s, x, a + 1:b + 1, :] + south * src[s, x, a - 1:b - 1, :]
                 + top * pltpu.roll(centre, 127, 1) + bottom * pltpu.roll(centre, 1, 1))
        return centre, total

    def smooth(src, dst, x):
        for t in range(3):
            faces = [cf[i, x, 8 * t:8 * t + 8, :] for i in range(6)]
            updated = []
            for s in range(8):
                centre, total = around(src, s, x, t, faces)
                updated.append(mk[s, x, 8 * t:8 * t + 8, :] * (0.5 * centre + total))
            whole = ((updated[0] + updated[1]) + (updated[2] + updated[3])) + (
                (updated[4] + updated[5]) + (updated[6] + updated[7]))
            scale = 1.0 / jnp.where(whole > 0.0, whole, 1.0)
            for s in range(8):
                dst[s, x, 8 + 8 * t:16 + 8 * t, :] = updated[s] * scale

    def apply(x):
        for t in range(3):
            faces = [cf[i, x, 8 * t:8 * t + 8, :] for i in range(6)]
            diagonal = cf[6, x, 8 * t:8 * t + 8, :]
            for s in range(8):
                centre, total = around(ba, s, x, t, faces)
                ap[s, x, 8 * t:8 * t + 8, :] = diagonal * (centre - total)

    def weigh(a):
        for i in range(5):
            x = SUM_START[a] + 4 + i
            for t in range(3):
                code = fe[CODE, x, 8 + 8 * t:16 + 8 * t, :].astype(jnp.int32)
                in_x = (((code >> 2) & 1) == a // 2).astype(F32)
                odd_y = ((code >> 1) & 1).astype(F32)
                odd_z = (code & 1).astype(F32)
                in_y = 1.0 - odd_y if t == 0 else odd_y
                wm[a * 5 + i, 0, 8 * t:8 * t + 8, :] = in_x
                wm[a * 5 + i, 1, 8 * t:8 * t + 8, :] = in_x * odd_z
                wm[a * 5 + i, 2, 8 * t:8 * t + 8, :] = in_x * in_y
                wm[a * 5 + i, 3, 8 * t:8 * t + 8, :] = in_x * in_y * odd_z

    def sums(a, s):
        for t in range(3):
            parts = [None] * 4
            for i in range(5):
                value = ap[s, SUM_START[a] + 4 + i, 8 * t:8 * t + 8, :]
                for m in range(4) if t == 1 else (2, 3):
                    if m == 0 and i not in SUM_MASKED[a]:
                        term = value
                    else:
                        term = value * wm[a * 5 + i, m, 8 * t:8 * t + 8, :]
                    parts[m] = term if parts[m] is None else parts[m] + term
            for m in range(4) if t == 1 else (2, 3):
                place = a * 8 + (m - 2 if t == 0 else m + 2 if t == 1 else m + 4)
                acc[pl.ds(pl.multiple_of((place * 8 + s) * 8, 8), 8), :] = parts[m]

    def over_rows(a):
        r = []
        for place in range(a * 8, a * 8 + 8):
            total = acc[pl.ds(place * 64, 8, stride=8), :]
            for y in range(1, 8):
                total = total + acc[pl.ds(place * 64 + y, 8, stride=8), :]
            r.append(total)
        r[2], r[3] = r[2] - r[4], r[3] - r[5]
        for b in range(4):
            for m in range(2):
                start = m * 128 + (a * 4 + b) * 8
                xs[start:start + 8, :] = r[2 * b + m]

    def layers(step, start, stop, unroll):
        def body(x, carry):
            step(x)
            return carry

        lax.fori_loop(start, stop, body, 0, unroll=unroll)

    def both(step, start, other, count, unroll):
        def body(i, carry):
            step(start + i)
            step(other + i)
            return carry

        lax.fori_loop(0, count, body, 0, unroll=unroll)

    def give(x):
        for s in range(8):
            pro[s, x] = ba[s, x + 4, 12:28, :]

    once = functools.partial(smooth, ba, bb)
    twice = functools.partial(smooth, bb, ba)

    layers(unpack, 4, 20, 8)
    layers(first, 4, 20, 8)
    layers(coefficients, 5, 20, 5)
    layers(once, 5, 19, 7)
    layers(twice, 6, 18, 6)
    layers(give, 2, 14, 4)
    layers(apply, 7, 17, 5)
    weigh(1)
    weigh(2)
    layers(functools.partial(sums, 1), 0, 8, 4)
    layers(functools.partial(sums, 2), 0, 8, 4)

    arrive(near_copies)
    for i in range(8):
        fe[i % 4, 2 + i // 4, 12:28, :] = rxl[6 + i]
        fe[i % 4, 20 + i // 4, 12:28, :] = rxh[i]
    for x in (2, 3, 20, 21):
        unpack(x)
    both(first, 2, 20, 2, 2)
    both(coefficients, 3, 20, 2, 2)
    both(once, 3, 19, 2, 2)
    both(twice, 4, 18, 2, 2)
    both(give, 0, 14, 2, 2)
    both(apply, 5, 17, 2, 2)
    weigh(0)
    weigh(3)

    arrive(deep_copies)
    for i in range(6):
        flat = 50 + i
        fe[flat % 4, flat // 4 - 12, 12:28, :] = rxl[i]
    for i in range(4):
        fe[i, 22, 12:28, :] = rxh[8 + i]
    fe[CODE, 23, 12:28, :] = rxh[12]
    for c, (dx, dy) in enumerate(CORNERS):
        a, b = (1, 0) if dx > 0 else (22, 23)
        y, edge = (10, 11) if dy > 0 else (28, 28)
        for k in range(4):
            fe[k, a, y:y + 2, :] = crx[c, 2 * k:2 * k + 2, :]
        fe[FX, b, edge:edge + 1, :] = crx[c, 8:9, :]
        fe[CODE, b, edge:edge + 1, :] = crx[c, 9:10, :]
    both(first, 0, 22, 2, 2)
    both(coefficients, 1, 22, 1, 1)
    coefficients(2)
    both(once, 1, 21, 2, 2)
    both(twice, 2, 20, 2, 2)
    both(apply, 3, 19, 2, 2)
    layers(functools.partial(sums, 0), 0, 8, 4)
    layers(functools.partial(sums, 3), 0, 8, 4)
    for a in range(4):
        over_rows(a)

    lane_tile = (iota((128, 128), 0) + 4) >> 3
    col = iota((128, 128), 1)
    even = (col & 1) == 0
    even_row = (iota((128, 128), 0) & 1) == 0
    halves = []
    for up in range(2):
        gather = ((lane_tile == col + up) & (col < 16)).astype(F32)
        z = dot_left(xs[...], gather)
        v = jnp.where(even, z[0:128] - z[128:256], z[128:256])
        other = jnp.where(even_row, pltpu.roll(v, 127, 0), pltpu.roll(v, 1, 0))
        halves.append(jnp.where(even, v, other))
    entries = dot(ct[:, 0:128], halves[0]) + dot(ct[:, 128:256], halves[1])
    routed = dot_nt(pp[0], entries[0:32])
    for b in range(1, 4):
        routed = routed + dot_nt(pp[b], entries[32 * b:32 * b + 32])
    snd[:, 0:32] = routed
    snd[:, 32:128] = jnp.zeros((128, 96), F32)

    mine = pl.multiple_of(gy * 8, 8)
    sent = []
    for j in range(1, n_y):
        there = lax.rem(gy + j, n_y)
        copy = remote(snd.at[pl.ds(pl.multiple_of(there * 8, 8), 8)], rcv.at[pl.ds(mine, 8)],
                      e_send.at[j], e_recv.at[j], 0, j)
        copy.start()
        sent.append(copy)
    rcv[pl.ds(mine, 8), :] = snd[pl.ds(mine, 8), :]
    for copy in sent:
        copy.wait_recv()
    rows[:, 0, :] = rcv[...].T[0:27, :]
    leave(pad_copies + y_copies + near_copies + deep_copies)
    for copy in sent:
        copy.wait_send()


def writer(pro, rows, pro_out, rows_out, sem):
    copies = [pltpu.make_async_copy(pro, pro_out, sem.at[0]), pltpu.make_async_copy(rows, rows_out, sem.at[1])]
    for copy in copies:
        copy.start()
    for copy in copies:
        copy.wait()


def solution(mesh):
    n_x, n_y = mesh.shape["gx"], mesh.shape["gy"]
    hbm = pl.BlockSpec(memory_space=pltpu.HBM)
    vmem = pl.BlockSpec(memory_space=pltpu.VMEM)
    dma = pltpu.SemaphoreType.DMA

    def on_device(face_trans, partition, support_pad, owners):
        prolongation, rows = pl.pallas_call(
            functools.partial(kernel, n_x, n_y),
            out_shape=(
                pltpu.VMEM((8, 16, 16, 128), F32),
                pltpu.VMEM((27, 1, 128), F32),
            ),
            in_specs=[hbm] * 4,
            out_specs=(vmem, vmem),
            scratch_shapes=[
                pltpu.VMEM((3, 16, 16, 128), F32),
                pltpu.VMEM((16, 16, 128), jnp.int32),
                pltpu.VMEM((6, 2, 2, 16), jnp.int32),
                pltpu.VMEM((1, 64), jnp.int32),
                pltpu.VMEM((64, 16, 128), F32),
                pltpu.VMEM((14, 16, 128), F32),
                pltpu.VMEM((13, 16, 128), F32),
                pltpu.VMEM((256, 128), F32),
                pltpu.VMEM((256, 128), F32),
                pltpu.VMEM((384, 128), F32),
                pltpu.VMEM((384, 128), F32),
                pltpu.VMEM((4, 16, 128), F32),
                pltpu.VMEM((4, 16, 128), F32),
                pltpu.VMEM((8, 128), F32),
                pltpu.VMEM((64, 128), F32),
                pltpu.VMEM((16, 128), F32),
                pltpu.VMEM((10, 16, 128), F32),
                pltpu.VMEM((8, 3, E, 128), F32),
                pltpu.VMEM((4, E, 40, 128), F32),
                pltpu.VMEM((7, E, E, 128), F32),
                pltpu.VMEM((8, E, E, 128), F32),
                pltpu.VMEM((8, E, 40, 128), F32),
                pltpu.VMEM((8, E, 40, 128), F32),
                pltpu.VMEM((8, E, E, 128), F32),
                pltpu.VMEM((20, 4, E, 128), F32),
                pltpu.VMEM((2048, 128), F32),
                pltpu.VMEM((256, 128), F32),
                pltpu.VMEM((128, 256), F32),
                pltpu.VMEM((4, 128, 128), F32),
                pltpu.VMEM((8, 128), F32),
                pltpu.VMEM((128, 128), F32),
                pltpu.VMEM((8 * n_y, 128), F32),
                dma((4,)), dma((5,)), dma((5,)), dma((10,)), dma((10,)), dma((8,)), dma((8,)), dma((n_y,)), dma((n_y,)),
            ],
            compiler_params=pltpu.CompilerParams(
                collective_id=0, has_side_effects=True, vmem_limit_bytes=48 * 2**20
            ),
        )(*(pltpu.with_memory_space_constraint(a, pltpu.HBM)
            for a in (face_trans, partition, support_pad, owners.reshape(1, 64))))
        prolongation, rows = pl.pallas_call(
            writer,
            out_shape=(
                jax.ShapeDtypeStruct((8, 16, 16, 128), F32),
                jax.ShapeDtypeStruct((27, 1, 128), F32),
            ),
            in_specs=[vmem] * 2,
            out_specs=(hbm, hbm),
            scratch_shapes=[dma((2,))],
        )(*(pltpu.with_memory_space_constraint(a, pltpu.VMEM) for a in (prolongation, rows)))
        return prolongation, rows.reshape(1, 1, 27, 128)

    placed = (
        P(None, "gx", "gy", None),
        P("gx", "gy", None),
        P(None, "gx", "gy", None),
        P("gx", "gy", None, None),
    )
    return jax.shard_map(
        on_device,
        mesh=mesh,
        in_specs=placed,
        out_specs=(P(None, "gx", "gy", None), P("gx", "gy", None, None)),
        check_vma=False,
    )
```

```python
import functools

import jax
import jax.numpy as jnp
from jax import lax
from jax.experimental import pallas as pl
from jax.experimental.pallas import tpu as pltpu
from jax.sharding import PartitionSpec as P

MESH = pl.DeviceIdType.MESH
F32 = jnp.float32

E = 24
FY, FZ, FX, CODE = range(4)
AROUND = [(dx, dy) for dx in (-1, 0, 1) for dy in (-1, 0, 1) if (dx, dy) != (0, 0)]
CORNERS = [(dx, dy) for dx in (1, -1) for dy in (1, -1)]
SUM_START = (-1, 4, 7, 12)
SUM_MASKED = ((0, 1), (3, 4), (0, 1), (3, 4))


def iota(shape, dim):
    return lax.broadcasted_iota(jnp.int32, shape, dim)


def parts(a):
    high = a.astype(jnp.bfloat16)
    rest = a - high.astype(F32)
    middle = rest.astype(jnp.bfloat16)
    return high, middle, (rest - middle.astype(F32)).astype(jnp.bfloat16)


def dot(a, b, dims=(((1,), (0,)), ((), ()))):
    total = None
    exact = a.astype(jnp.bfloat16)
    for part in parts(b):
        term = lax.dot_general(exact, part, dims, preferred_element_type=F32)
        total = term if total is None else total + term
    return total


def dot_left(a, b):
    total = None
    exact = b.astype(jnp.bfloat16)
    for part in parts(a):
        term = lax.dot_general(part, exact, (((1,), (0,)), ((), ())), preferred_element_type=F32)
        total = term if total is None else total + term
    return total


def dot_nt(a, b):
    return dot(a, b, (((1,), (1,)), ((), ())))


def kernel(n_x, n_y, ft_in, pt_in, sp_in, ow_in, pro, rows,
           ft, pt, sp, ow, own, rxl, rxh, ypl, yph, ryl, ryh, cpk, crx, pd, rp, pe, ex, yz, fe, cf, mk, ba, bb, ap, wm, acc, xs, ct, pp, orow,
           snd, rcv, in_sem, x_send, x_recv, y_send, y_recv, p_send, p_recv, e_send, e_recv):
    gx = lax.axis_index("gx")
    gy = lax.axis_index("gy")
    peer = lambda dx, dy: (lax.rem(gx + (dx + n_x), n_x), lax.rem(gy + (dy + n_y), n_y))

    barrier = pltpu.get_barrier_semaphore()
    far = [j for j in range(1, n_y) if j not in (1, n_y - 1)]

    def inside(dx, dy):
        fits = None
        for d, at, count in ((dx, gx, n_x), (dy, gy, n_y)):
            if d:
                part = at > 0 if d < 0 else at < count - 1
                fits = part if fits is None else fits & part
        return fits

    for dx, dy in AROUND:
        def greet(dx=dx, dy=dy):
            pl.semaphore_signal(barrier, inc=1, device_id=peer(dx, dy), device_id_type=MESH)

        if dx == 0:
            greet()
        else:
            pl.when(inside(dx, dy))(greet)
    for j in far:
        pl.semaphore_signal(barrier, inc=1, device_id=peer(0, j), device_id_type=MESH)

    loads = [
        pltpu.make_async_copy(src, dst, in_sem.at[i])
        for i, (src, dst) in enumerate(((ft_in, ft), (pt_in, pt), (sp_in, sp), (ow_in, ow)))
    ]
    for copy in loads:
        copy.start()

    zero8 = jnp.zeros((8, 128), F32)

    def clear(x, carry):
        for s in range(8):
            for b in (ba, bb):
                b[s, x, 0:8, :] = zero8
                b[s, x, 32:40, :] = zero8
        for k in range(4):
            fe[k, x, 0:8, :] = zero8
        return carry

    lax.fori_loop(0, E, clear, 0)
    for c in range(4):
        cpk[c, 8:16, :] = zero8
    for x in (0, 1, 22, 23):
        for k in range(4):
            fe[k, x, 8:16, :] = jnp.ones((8, 128), F32)
            fe[k, x, 24:32, :] = jnp.ones((8, 128), F32)
    for copy in loads:
        copy.wait()

    pd[...] = jnp.zeros((8, 128), F32)
    for bx in range(2):
        total = None
        for k in range(6):
            place = (iota((16, 128), 1) == iota((16, 128), 0) + 16 * k).astype(F32)
            term = dot(sp[k, bx].astype(F32), place)
            total = term if total is None else total + term
        pd[2 * bx:2 * bx + 2, :] = total

    x_last = gx == n_x - 1
    y_last = gy == n_y - 1
    row16 = iota((16, 128), 0)
    lane16 = iota((16, 128), 1)
    keep_y = jnp.where((row16 == 15) & y_last, 0.0, 1.0)
    keep_z = jnp.where(lane16 == 127, 0.0, 1.0)

    def stage(x, carry):
        keep_x = jnp.where((x == 15) & x_last, 0.0, 1.0)
        p = pt[x]
        px = (p >= 9).astype(jnp.int32) + (p >= 18).astype(jnp.int32)
        q = p - 9 * px
        py = (q >= 3).astype(jnp.int32) + (q >= 6).astype(jnp.int32)
        pz = q - 3 * py
        bx = ((x >> 3) + px + 1) & 1
        by = ((row16 >> 3) + py + 1) & 1
        bz = ((lane16 >> 3) + pz + 1) & 1
        code = (4 * bx + 2 * by + bz).astype(F32)
        values = {FX: ft[0, x] * keep_x, FY: ft[1, x] * keep_y, FZ: ft[2, x] * keep_z, CODE: code}
        for k in range(4):
            own[x * 4 + k] = values[k]
            fe[k, x + 4, 12:28, :] = values[k]
            start = pl.multiple_of(x * 16, 8) + 4 * k
            ypl[pl.ds(start, 4), :] = values[k][0:4]
            yph[pl.ds(start, 4), :] = values[k][12:16]
        return carry

    lax.fori_loop(0, 16, stage, 0)
    for c, (dx, dy) in enumerate(CORNERS):
        a, b = (13, 12) if dx > 0 else (2, 3)
        y, edge = (14, 15) if dy > 0 else (0, 0)
        for k in range(4):
            cpk[c, 2 * k:2 * k + 2, :] = own[a * 4 + k, y:y + 2, :]
        cpk[c, 8:9, :] = own[b * 4 + FX, edge:edge + 1, :]
        cpk[c, 9:10, :] = own[b * 4 + CODE, edge:edge + 1, :]
    sides_x = 2 - (gx == 0).astype(jnp.int32) - x_last.astype(jnp.int32)
    sides_y = 2 - (gy == 0).astype(jnp.int32) - y_last.astype(jnp.int32)
    pl.semaphore_wait(barrier, 2 + len(far) + sides_x * (1 + sides_y))

    def remote(src, dst, send, recv, dx, dy):
        return pltpu.make_async_remote_copy(src_ref=src, dst_ref=dst, send_sem=send, recv_sem=recv,
                                            device_id=peer(dx, dy), device_id_type=MESH)

    def between(act, copies, sign=1):
        for (dx, dy), copy in copies:
            pl.when(inside(sign * dx, sign * dy))(functools.partial(act, copy))

    def start(copies):
        between(lambda copy: copy.start(), copies)

    def arrive(copies):
        between(lambda copy: copy.wait_recv(), copies, -1)

    def leave(copies):
        between(lambda copy: copy.wait_send(), copies)

    def link(src, dst, send, recv, dx, dy):
        return (dx, dy), remote(src, dst, send, recv, dx, dy)

    pad_copies = [
        link(pd, rp.at[pl.ds(8 * d, 8)], p_send.at[d], p_recv.at[d], dx, dy) for d, (dx, dy) in enumerate(AROUND)
    ]
    y_copies = [
        link(yph, ryl.at[pl.ds(64, 256)], y_send.at[0], y_recv.at[0], 0, 1),
        link(ypl, ryh.at[pl.ds(64, 256)], y_send.at[1], y_recv.at[1], 0, -1),
    ]
    near_copies = [
        link(own.at[pl.ds(56, 8)], rxl.at[pl.ds(6, 8)], x_send.at[0], x_recv.at[0], 1, 0),
        link(own.at[pl.ds(0, 8)], rxh.at[pl.ds(0, 8)], x_send.at[1], x_recv.at[1], -1, 0),
    ]
    deep_copies = [
        link(own.at[pl.ds(50, 6)], rxl.at[pl.ds(0, 6)], x_send.at[2], x_recv.at[2], 1, 0),
        link(own.at[pl.ds(8, 4)], rxh.at[pl.ds(8, 4)], x_send.at[3], x_recv.at[3], -1, 0),
        link(own.at[pl.ds(15, 1)], rxh.at[pl.ds(12, 1)], x_send.at[4], x_recv.at[4], -1, 0),
    ]
    near_corners, deep_corners = [], []
    for c, (dx, dy) in enumerate(CORNERS):
        src, dst = (yph, ryl) if dy > 0 else (ypl, ryh)
        a, b = (224, 32) if dx > 0 else (0, 320)
        near_corners.append(
            link(src.at[pl.ds(a, 32)], dst.at[pl.ds(b, 32)], y_send.at[2 + c], y_recv.at[2 + c], dx, dy))
        deep_corners.append(link(cpk.at[c], crx.at[c], y_send.at[6 + c], y_recv.at[6 + c], dx, dy))
    start(near_copies)
    start(pad_copies)
    start(y_copies)
    start(near_corners)
    start(deep_copies)
    start(deep_corners)

    for (dx, dy), c in zip(CORNERS, range(4)):
        def fill(c=c, dy=dy):
            crx[c] = jnp.ones((16, 128), F32)
            if dy > 0:
                crx[c, 2 * FY + 1:2 * FY + 2, :] = jnp.zeros((1, 128), F32)

        pl.when(jnp.logical_not(inside(-dx, -dy)))(fill)

    near_copies += near_corners
    deep_copies += deep_corners

    def beyond(ref, layers_of_x, code):
        for x in layers_of_x:
            ref[16 * x:16 * x + 16, :] = jnp.ones((16, 128), F32)
            ref[16 * x + 4 * CODE:16 * x + 4 * CODE + 4, :] = jnp.full((4, 128), code, F32)

    def closed_west():
        for r in (ryl, ryh):
            r[48 + 4 * FX:52 + 4 * FX, :] = jnp.zeros((4, 128), F32)

    @pl.when(gx == 0)
    def _():
        for i in range(14):
            k = (50 + i) % 4
            rxl[i] = jnp.full((16, 128), 6.0 if k == CODE else 0.0 if (k, i) == (FX, 12) else 1.0, F32)
        beyond(ryl, range(4), 6.0)
        beyond(ryh, range(4), 6.0)
        closed_west()

    @pl.when(x_last)
    def _():
        rxh[...] = jnp.ones_like(rxh)
        beyond(ryl, range(20, 24), 1.0)
        beyond(ryh, range(20, 24), 1.0)

    @pl.when(gy == 0)
    def _():
        beyond(ryl, range(E), 6.0)
        for x in range(E):
            ryl[16 * x + 4 * FY + 3:16 * x + 4 * FY + 4, :] = jnp.zeros((1, 128), F32)
        pl.when(gx == 0)(closed_west)

    @pl.when(y_last)
    def _():
        beyond(ryh, range(E), 1.0)
        pl.when(gx == 0)(closed_west)

    orow[...] = jnp.full((8, 128), -1.0, F32)
    orow[0:1, 0:64] = ow[...].astype(F32)
    owner = jnp.broadcast_to(orow[0:1, :], (128, 128))
    earlier = (owner == owner.T) & (iota((128, 128), 0) < iota((128, 128), 1))
    rank = jnp.sum(earlier.astype(F32), axis=0, keepdims=True)
    target = orow[0:1, :] * 8.0 + rank
    row_f = iota((128, 128), 0).astype(F32)
    for b in range(4):
        shifted = jnp.broadcast_to(target, (8, 128))
        if b:
            shifted = pltpu.roll(shifted, 128 - 16 * b, 1)
        pp[b] = ((row_f == shifted[0:1]) & (iota((128, 128), 1) < 16)).astype(F32)

    c = iota((128, 256), 1)
    up_z, b_x, up_x, b_y, up_y = c >> 7, (c >> 6) & 1, (c >> 5) & 1, (c >> 4) & 1, (c >> 3) & 1
    s_x, s_y, s_z = (c >> 2) & 1, (c >> 1) & 1, c & 1
    o_x = jnp.where(s_x == b_x, 1, 2 * up_x)
    o_y = jnp.where(s_y == b_y, 1, 2 * up_y)
    o_z = jnp.where(s_z == 0, 1, 2 * up_z)
    ct[...] = (iota((128, 256), 0) == (b_x * 2 + b_y) * 32 + 9 * o_x + 3 * o_y + o_z).astype(F32)

    arrive(pad_copies)
    low = {-1: 0, 0: 1, 1: 3}
    for dx, dy in AROUND + [(0, 0)]:
        sx, sy = -dx, -dy
        base = 0 if (dx, dy) == (0, 0) else 8 * AROUND.index((dx, dy))
        src = pd if (dx, dy) == (0, 0) else rp
        for i in ((1,) if sx < 0 else (0,) if sx > 0 else (0, 1)):
            for j in ((1,) if sy < 0 else (0,) if sy > 0 else (0, 1)):
                bi = low[sx] + (i if sx == 0 else 0)
                bj = low[sy] + (j if sy == 0 else 0)
                pe[4 * bi + bj:4 * bi + bj + 1, :] = src[base + 2 * i + j:base + 2 * i + j + 1, :]
    block_row = iota((16, 128), 0)
    outside = ((((block_row >> 2) == 0) & (gx == 0)) | (((block_row >> 2) == 3) & x_last)
               | (((block_row & 3) == 0) & (gy == 0)) | (((block_row & 3) == 3) & y_last))
    pads = jnp.where(outside, 0.0, pe[...])
    r_in = iota((128, 128), 0)
    tile_z = (iota((128, 128), 1) + 4) >> 3
    for sz in range(2):
        upper = (tile_z & 1) == sz
        bz = jnp.where(upper, tile_z, tile_z - 1)
        fits = (bz >= 0) & (bz < 16)
        for k in range(5):
            lanes = bz + 16 * k if k < 4 else bz + jnp.where(upper, 64, 80)
            ex[sz * 5 + k] = dot(pads, (fits & (r_in == lanes)).astype(F32))

    row8 = iota((8, 128), 0).astype(F32)
    lane8 = iota((8, 128), 1)
    i_z = ((lane8 + 4) & 7).astype(F32)
    up8 = ((lane8 + 4) >> 3) & 1
    for s in range(8):
        sx, sy, sz = s >> 2, (s >> 1) & 1, s & 1
        for g in range(3):
            bx = g if g % 2 == sx else g - 1
            for t in range(3):
                by = t if t % 2 == sy else t - 1
                r = (bx + 1) * 4 + by + 1
                reach_z = ex[sz * 5 + 4, r:r + 1, :]
                ok_z = jnp.where(up8 == sz, i_z + reach_z, 7.0 - i_z + reach_z) >= 4.0
                if by == t:
                    ok_y = row8 + ex[sz * 5 + 2, r:r + 1, :] >= 4.0
                else:
                    ok_y = row8 <= 3.0 + ex[sz * 5 + 3, r:r + 1, :]
                yz[s, g, 8 * t:8 * t + 8, :] = (ok_z & ok_y).astype(F32)

    def masks(i, carry):
        at = i.astype(F32)
        for s in range(8):
            sx, sy, sz = s >> 2, (s >> 1) & 1, s & 1
            for g in range(3):
                bx = g if g % 2 == sx else g - 1
                for t in range(3):
                    by = t if t % 2 == sy else t - 1
                    r = (bx + 1) * 4 + by + 1
                    if bx == g:
                        ok_x = ex[sz * 5, r:r + 1, :] >= 4.0 - at
                    else:
                        ok_x = ex[sz * 5 + 1, r:r + 1, :] >= at - 3.0
                    mk[s, 8 * g + i, 8 * t:8 * t + 8, :] = jnp.where(ok_x, yz[s, g, 8 * t:8 * t + 8, :], 0.0)
        return carry

    lax.fori_loop(0, 8, masks, 0, unroll=4)

    arrive(y_copies)

    def unpack(x):
        for k in range(4):
            start = 16 * x + 4 * k
            if not isinstance(x, int):
                start = pl.multiple_of(x * 16, 8) + 4 * k
            fe[k, x, 8:12, :] = ryl[pl.ds(start, 4), :]
            fe[k, x, 28:32, :] = ryh[pl.ds(start, 4), :]

    def first(x):
        for t in range(3):
            code = fe[CODE, x, 8 + 8 * t:16 + 8 * t, :]
            for s in range(8):
                ba[s, x, 8 + 8 * t:16 + 8 * t, :] = (code == float(s)).astype(F32)

    def coefficients(x):
        for t in range(3):
            a, b = 8 + 8 * t, 16 + 8 * t
            east, west = fe[FX, x, a:b, :], fe[FX, x - 1, a:b, :]
            north, south = fe[FY, x, a:b, :], fe[FY, x, a - 1:b - 1, :]
            top = fe[FZ, x, a:b, :]
            bottom = pltpu.roll(top, 1, 1)
            diagonal = west + east + south + north + bottom + top
            inverse = 1.0 / diagonal
            for i, face in enumerate((east, west, north, south, top, bottom)):
                cf[i, x, 8 * t:8 * t + 8, :] = face * inverse
            cf[6, x, 8 * t:8 * t + 8, :] = diagonal

    def around(src, s, x, t, faces):
        east, west, north, south, top, bottom = faces
        a, b = 8 + 8 * t, 16 + 8 * t
        centre = src[s, x, a:b, :]
        total = (east * src[s, x + 1, a:b, :] + west * src[s, x - 1, a:b, :]
                 + north * src[s, x, a + 1:b + 1, :] + south * src[s, x, a - 1:b - 1, :]
                 + top * pltpu.roll(centre, 127, 1) + bottom * pltpu.roll(centre, 1, 1))
        return centre, total

    def smooth(src, dst, x):
        for t in range(3):
            faces = [cf[i, x, 8 * t:8 * t + 8, :] for i in range(6)]
            updated = []
            for s in range(8):
                centre, total = around(src, s, x, t, faces)
                updated.append(mk[s, x, 8 * t:8 * t + 8, :] * (0.5 * centre + total))
            whole = ((updated[0] + updated[1]) + (updated[2] + updated[3])) + (
                (updated[4] + updated[5]) + (updated[6] + updated[7]))
            scale = 1.0 / jnp.where(whole > 0.0, whole, 1.0)
            for s in range(8):
                dst[s, x, 8 + 8 * t:16 + 8 * t, :] = updated[s] * scale

    def apply(x):
        for t in range(3):
            faces = [cf[i, x, 8 * t:8 * t + 8, :] for i in range(6)]
            diagonal = cf[6, x, 8 * t:8 * t + 8, :]
            for s in range(8):
                centre, total = around(ba, s, x, t, faces)
                ap[s, x, 8 * t:8 * t + 8, :] = diagonal * (centre - total)

    def weigh(a):
        for i in range(5):
            x = SUM_START[a] + 4 + i
            for t in range(3):
                code = fe[CODE, x, 8 + 8 * t:16 + 8 * t, :].astype(jnp.int32)
                in_x = (((code >> 2) & 1) == a // 2).astype(F32)
                odd_y = ((code >> 1) & 1).astype(F32)
                odd_z = (code & 1).astype(F32)
                in_y = 1.0 - odd_y if t == 0 else odd_y
                wm[a * 5 + i, 0, 8 * t:8 * t + 8, :] = in_x
                wm[a * 5 + i, 1, 8 * t:8 * t + 8, :] = in_x * odd_z
                wm[a * 5 + i, 2, 8 * t:8 * t + 8, :] = in_x * in_y
                wm[a * 5 + i, 3, 8 * t:8 * t + 8, :] = in_x * in_y * odd_z

    def sums(a, s):
        for t in range(3):
            parts = [None] * 4
            for i in range(5):
                value = ap[s, SUM_START[a] + 4 + i, 8 * t:8 * t + 8, :]
                for m in range(4) if t == 1 else (2, 3):
                    if m == 0 and i not in SUM_MASKED[a]:
                        term = value
                    else:
                        term = value * wm[a * 5 + i, m, 8 * t:8 * t + 8, :]
                    parts[m] = term if parts[m] is None else parts[m] + term
            for m in range(4) if t == 1 else (2, 3):
                place = a * 8 + (m - 2 if t == 0 else m + 2 if t == 1 else m + 4)
                acc[pl.ds(pl.multiple_of((place * 8 + s) * 8, 8), 8), :] = parts[m]

    def over_rows(a):
        r = []
        for place in range(a * 8, a * 8 + 8):
            total = acc[pl.ds(place * 64, 8, stride=8), :]
            for y in range(1, 8):
                total = total + acc[pl.ds(place * 64 + y, 8, stride=8), :]
            r.append(total)
        r[2], r[3] = r[2] - r[4], r[3] - r[5]
        for b in range(4):
            for m in range(2):
                start = m * 128 + (a * 4 + b) * 8
                xs[start:start + 8, :] = r[2 * b + m]

    def layers(step, start, stop, unroll):
        def body(x, carry):
            step(x)
            return carry

        lax.fori_loop(start, stop, body, 0, unroll=unroll)

    def both(step, start, other, count, unroll):
        def body(i, carry):
            step(start + i)
            step(other + i)
            return carry

        lax.fori_loop(0, count, body, 0, unroll=unroll)

    def give(x):
        for s in range(8):
            pro[s, x] = ba[s, x + 4, 12:28, :]

    once = functools.partial(smooth, ba, bb)
    twice = functools.partial(smooth, bb, ba)

    layers(unpack, 4, 20, 8)
    layers(first, 4, 20, 8)
    layers(coefficients, 5, 20, 5)
    layers(once, 5, 19, 7)
    layers(twice, 6, 18, 6)
    layers(give, 2, 14, 4)
    layers(apply, 7, 17, 5)
    weigh(1)
    weigh(2)
    layers(functools.partial(sums, 1), 0, 8, 4)
    layers(functools.partial(sums, 2), 0, 8, 4)
    over_rows(1)
    over_rows(2)

    arrive(near_copies)
    for i in range(8):
        fe[i % 4, 2 + i // 4, 12:28, :] = rxl[6 + i]
        fe[i % 4, 20 + i // 4, 12:28, :] = rxh[i]
    for x in (2, 3, 20, 21):
        unpack(x)
    both(first, 2, 20, 2, 2)
    both(coefficients, 3, 20, 2, 2)
    both(once, 3, 19, 2, 2)
    both(twice, 4, 18, 2, 2)
    both(give, 0, 14, 2, 2)
    both(apply, 5, 17, 2, 2)
    weigh(0)
    weigh(3)

    arrive(deep_copies)
    for i in range(6):
        flat = 50 + i
        fe[flat % 4, flat // 4 - 12, 12:28, :] = rxl[i]
    for i in range(4):
        fe[i, 22, 12:28, :] = rxh[8 + i]
    fe[CODE, 23, 12:28, :] = rxh[12]
    for c, (dx, dy) in enumerate(CORNERS):
        a, b = (1, 0) if dx > 0 else (22, 23)
        y, edge = (10, 11) if dy > 0 else (28, 28)
        for k in range(4):
            fe[k, a, y:y + 2, :] = crx[c, 2 * k:2 * k + 2, :]
        fe[FX, b, edge:edge + 1, :] = crx[c, 8:9, :]
        fe[CODE, b, edge:edge + 1, :] = crx[c, 9:10, :]
    both(first, 0, 22, 2, 2)
    both(coefficients, 1, 22, 1, 1)
    coefficients(2)
    both(once, 1, 21, 2, 2)
    both(twice, 2, 20, 2, 2)
    both(apply, 3, 19, 2, 2)
    layers(functools.partial(sums, 0), 0, 8, 4)
    layers(functools.partial(sums, 3), 0, 8, 4)
    over_rows(0)
    over_rows(3)

    lane_tile = (iota((128, 128), 0) + 4) >> 3
    col = iota((128, 128), 1)
    even = (col & 1) == 0
    even_row = (iota((128, 128), 0) & 1) == 0
    halves = []
    for up in range(2):
        gather = ((lane_tile == col + up) & (col < 16)).astype(F32)
        z = dot_left(xs[...], gather)
        v = jnp.where(even, z[0:128] - z[128:256], z[128:256])
        other = jnp.where(even_row, pltpu.roll(v, 127, 0), pltpu.roll(v, 1, 0))
        halves.append(jnp.where(even, v, other))
    entries = dot(ct[:, 0:128], halves[0]) + dot(ct[:, 128:256], halves[1])
    routed = dot_nt(pp[0], entries[0:32])
    for b in range(1, 4):
        routed = routed + dot_nt(pp[b], entries[32 * b:32 * b + 32])
    snd[:, 0:32] = routed
    snd[:, 32:128] = jnp.zeros((128, 96), F32)

    mine = pl.multiple_of(gy * 8, 8)
    sent = []
    for j in sorted(range(1, n_y), key=lambda j: abs(2 * j - n_y)):
        there = lax.rem(gy + j, n_y)
        copy = remote(snd.at[pl.ds(pl.multiple_of(there * 8, 8), 8)], rcv.at[pl.ds(mine, 8)],
                      e_send.at[j], e_recv.at[j], 0, j)
        copy.start()
        sent.append(copy)
    rcv[pl.ds(mine, 8), :] = snd[pl.ds(mine, 8), :]
    for copy in sent:
        copy.wait_recv()
    rows[:, 0, :] = rcv[...].T[0:27, :]
    leave(pad_copies + y_copies + near_copies + deep_copies)
    for copy in sent:
        copy.wait_send()


def writer(pro, rows, pro_out, rows_out, sem):
    copies = [pltpu.make_async_copy(pro, pro_out, sem.at[0]), pltpu.make_async_copy(rows, rows_out, sem.at[1])]
    for copy in copies:
        copy.start()
    for copy in copies:
        copy.wait()


def solution(mesh):
    n_x, n_y = mesh.shape["gx"], mesh.shape["gy"]
    hbm = pl.BlockSpec(memory_space=pltpu.HBM)
    vmem = pl.BlockSpec(memory_space=pltpu.VMEM)
    dma = pltpu.SemaphoreType.DMA

    def on_device(face_trans, partition, support_pad, owners):
        prolongation, rows = pl.pallas_call(
            functools.partial(kernel, n_x, n_y),
            out_shape=(
                pltpu.VMEM((8, 16, 16, 128), F32),
                pltpu.VMEM((27, 1, 128), F32),
            ),
            in_specs=[hbm] * 4,
            out_specs=(vmem, vmem),
            scratch_shapes=[
                pltpu.VMEM((3, 16, 16, 128), F32),
                pltpu.VMEM((16, 16, 128), jnp.int32),
                pltpu.VMEM((6, 2, 2, 16), jnp.int32),
                pltpu.VMEM((1, 64), jnp.int32),
                pltpu.VMEM((64, 16, 128), F32),
                pltpu.VMEM((14, 16, 128), F32),
                pltpu.VMEM((13, 16, 128), F32),
                pltpu.VMEM((256, 128), F32),
                pltpu.VMEM((256, 128), F32),
                pltpu.VMEM((384, 128), F32),
                pltpu.VMEM((384, 128), F32),
                pltpu.VMEM((4, 16, 128), F32),
                pltpu.VMEM((4, 16, 128), F32),
                pltpu.VMEM((8, 128), F32),
                pltpu.VMEM((64, 128), F32),
                pltpu.VMEM((16, 128), F32),
                pltpu.VMEM((10, 16, 128), F32),
                pltpu.VMEM((8, 3, E, 128), F32),
                pltpu.VMEM((4, E, 40, 128), F32),
                pltpu.VMEM((7, E, E, 128), F32),
                pltpu.VMEM((8, E, E, 128), F32),
                pltpu.VMEM((8, E, 40, 128), F32),
                pltpu.VMEM((8, E, 40, 128), F32),
                pltpu.VMEM((8, E, E, 128), F32),
                pltpu.VMEM((20, 4, E, 128), F32),
                pltpu.VMEM((2048, 128), F32),
                pltpu.VMEM((256, 128), F32),
                pltpu.VMEM((128, 256), F32),
                pltpu.VMEM((4, 128, 128), F32),
                pltpu.VMEM((8, 128), F32),
                pltpu.VMEM((128, 128), F32),
                pltpu.VMEM((8 * n_y, 128), F32),
                dma((4,)), dma((5,)), dma((5,)), dma((10,)), dma((10,)), dma((8,)), dma((8,)), dma((n_y,)), dma((n_y,)),
            ],
            compiler_params=pltpu.CompilerParams(
                collective_id=0, has_side_effects=True, vmem_limit_bytes=48 * 2**20
            ),
        )(*(pltpu.with_memory_space_constraint(a, pltpu.HBM)
            for a in (face_trans, partition, support_pad, owners.reshape(1, 64))))
        prolongation, rows = pl.pallas_call(
            writer,
            out_shape=(
                jax.ShapeDtypeStruct((8, 16, 16, 128), F32),
                jax.ShapeDtypeStruct((27, 1, 128), F32),
            ),
            in_specs=[vmem] * 2,
            out_specs=(hbm, hbm),
            scratch_shapes=[dma((2,))],
        )(*(pltpu.with_memory_space_constraint(a, pltpu.VMEM) for a in (prolongation, rows)))
        return prolongation, rows.reshape(1, 1, 27, 128)

    placed = (
        P(None, "gx", "gy", None),
        P("gx", "gy", None),
        P(None, "gx", "gy", None),
        P("gx", "gy", None, None),
    )
    return jax.shard_map(
        on_device,
        mesh=mesh,
        in_specs=placed,
        out_specs=(P(None, "gx", "gy", None), P("gx", "gy", None, None)),
        check_vma=False,
    )
```

```python
import functools

import jax
import jax.numpy as jnp
from jax import lax
from jax.experimental import pallas as pl
from jax.experimental.pallas import tpu as pltpu
from jax.sharding import PartitionSpec as P

MESH = pl.DeviceIdType.MESH
F32 = jnp.float32

E = 24
FY, FZ, FX, CODE = range(4)
AROUND = [(dx, dy) for dx in (-1, 0, 1) for dy in (-1, 0, 1) if (dx, dy) != (0, 0)]
CORNERS = [(dx, dy) for dx in (1, -1) for dy in (1, -1)]
SUM_START = (-1, 4, 7, 12)
SUM_MASKED = ((0, 1), (3, 4), (0, 1), (3, 4))


def iota(shape, dim):
    return lax.broadcasted_iota(jnp.int32, shape, dim)


def parts(a):
    high = a.astype(jnp.bfloat16)
    rest = a - high.astype(F32)
    middle = rest.astype(jnp.bfloat16)
    return high, middle, (rest - middle.astype(F32)).astype(jnp.bfloat16)


def dot(a, b, dims=(((1,), (0,)), ((), ()))):
    total = None
    exact = a.astype(jnp.bfloat16)
    for part in parts(b):
        term = lax.dot_general(exact, part, dims, preferred_element_type=F32)
        total = term if total is None else total + term
    return total


def dot_left(a, b):
    total = None
    exact = b.astype(jnp.bfloat16)
    for part in parts(a):
        term = lax.dot_general(part, exact, (((1,), (0,)), ((), ())), preferred_element_type=F32)
        total = term if total is None else total + term
    return total


def dot_nt(a, b):
    return dot(a, b, (((1,), (1,)), ((), ())))


def kernel(n_x, n_y, ft_in, pt_in, sp_in, ow_in, pro, rows,
           ft, pt, sp, ow, own, rxl, rxh, ypl, yph, ryl, ryh, cpk, crx, pd, rp, pe, ex, yz, fe, cf, mk, ba, bb, ap, wm, acc, xs, ct, pp, orow,
           snd, rcv, in_sem, x_send, x_recv, y_send, y_recv, p_send, p_recv, e_send, e_recv):
    gx = lax.axis_index("gx")
    gy = lax.axis_index("gy")
    peer = lambda dx, dy: (lax.rem(gx + (dx + n_x), n_x), lax.rem(gy + (dy + n_y), n_y))

    barrier = pltpu.get_barrier_semaphore()
    far = [j for j in range(1, n_y) if j not in (1, n_y - 1)]

    def inside(dx, dy):
        fits = None
        for d, at, count in ((dx, gx, n_x), (dy, gy, n_y)):
            if d:
                part = at > 0 if d < 0 else at < count - 1
                fits = part if fits is None else fits & part
        return fits

    for dx, dy in AROUND:
        def greet(dx=dx, dy=dy):
            pl.semaphore_signal(barrier, inc=1, device_id=peer(dx, dy), device_id_type=MESH)

        if dx == 0:
            greet()
        else:
            pl.when(inside(dx, dy))(greet)
    for j in far:
        pl.semaphore_signal(barrier, inc=1, device_id=peer(0, j), device_id_type=MESH)

    loads = [
        pltpu.make_async_copy(src, dst, in_sem.at[i])
        for i, (src, dst) in enumerate(((ft_in, ft), (pt_in, pt), (sp_in, sp), (ow_in, ow)))
    ]
    for copy in loads:
        copy.start()

    zero8 = jnp.zeros((8, 128), F32)

    def clear(x, carry):
        for s in range(8):
            for b in (ba, bb):
                b[s, x, 0:8, :] = zero8
                b[s, x, 32:40, :] = zero8
        for k in range(4):
            fe[k, x, 0:8, :] = zero8
        return carry

    lax.fori_loop(0, E, clear, 0)
    for c in range(4):
        cpk[c, 8:16, :] = zero8
    for x in (0, 1, 22, 23):
        for k in range(4):
            fe[k, x, 8:16, :] = jnp.ones((8, 128), F32)
            fe[k, x, 24:32, :] = jnp.ones((8, 128), F32)
    for copy in loads:
        copy.wait()

    pd[...] = jnp.zeros((8, 128), F32)
    for bx in range(2):
        total = None
        for k in range(6):
            place = (iota((16, 128), 1) == iota((16, 128), 0) + 16 * k).astype(F32)
            term = dot(sp[k, bx].astype(F32), place)
            total = term if total is None else total + term
        pd[2 * bx:2 * bx + 2, :] = total

    x_last = gx == n_x - 1
    y_last = gy == n_y - 1
    row16 = iota((16, 128), 0)
    lane16 = iota((16, 128), 1)
    keep_y = jnp.where((row16 == 15) & y_last, 0.0, 1.0)
    keep_z = jnp.where(lane16 == 127, 0.0, 1.0)

    def stage(x, carry):
        keep_x = jnp.where((x == 15) & x_last, 0.0, 1.0)
        p = pt[x]
        px = (p >= 9).astype(jnp.int32) + (p >= 18).astype(jnp.int32)
        q = p - 9 * px
        py = (q >= 3).astype(jnp.int32) + (q >= 6).astype(jnp.int32)
        pz = q - 3 * py
        bx = ((x >> 3) + px + 1) & 1
        by = ((row16 >> 3) + py + 1) & 1
        bz = ((lane16 >> 3) + pz + 1) & 1
        code = (4 * bx + 2 * by + bz).astype(F32)
        values = {FX: ft[0, x] * keep_x, FY: ft[1, x] * keep_y, FZ: ft[2, x] * keep_z, CODE: code}
        for k in range(4):
            own[x * 4 + k] = values[k]
            fe[k, x + 4, 12:28, :] = values[k]
            start = pl.multiple_of(x * 16, 8) + 4 * k
            ypl[pl.ds(start, 4), :] = values[k][0:4]
            yph[pl.ds(start, 4), :] = values[k][12:16]
        return carry

    lax.fori_loop(0, 16, stage, 0)
    for c, (dx, dy) in enumerate(CORNERS):
        a, b = (13, 12) if dx > 0 else (2, 3)
        y, edge = (14, 15) if dy > 0 else (0, 0)
        for k in range(4):
            cpk[c, 2 * k:2 * k + 2, :] = own[a * 4 + k, y:y + 2, :]
        cpk[c, 8:9, :] = own[b * 4 + FX, edge:edge + 1, :]
        cpk[c, 9:10, :] = own[b * 4 + CODE, edge:edge + 1, :]
    sides_x = 2 - (gx == 0).astype(jnp.int32) - x_last.astype(jnp.int32)
    sides_y = 2 - (gy == 0).astype(jnp.int32) - y_last.astype(jnp.int32)
    pl.semaphore_wait(barrier, 2 + len(far) + sides_x * (1 + sides_y))

    def remote(src, dst, send, recv, dx, dy):
        return pltpu.make_async_remote_copy(src_ref=src, dst_ref=dst, send_sem=send, recv_sem=recv,
                                            device_id=peer(dx, dy), device_id_type=MESH)

    def between(act, copies, sign=1):
        for (dx, dy), copy in copies:
            pl.when(inside(sign * dx, sign * dy))(functools.partial(act, copy))

    def start(copies):
        between(lambda copy: copy.start(), copies)

    def arrive(copies):
        between(lambda copy: copy.wait_recv(), copies, -1)

    def leave(copies):
        between(lambda copy: copy.wait_send(), copies)

    def link(src, dst, send, recv, dx, dy):
        return (dx, dy), remote(src, dst, send, recv, dx, dy)

    pad_copies = [
        link(pd, rp.at[pl.ds(8 * d, 8)], p_send.at[d], p_recv.at[d], dx, dy) for d, (dx, dy) in enumerate(AROUND)
    ]
    y_copies = [
        link(yph, ryl.at[pl.ds(64, 256)], y_send.at[0], y_recv.at[0], 0, 1),
        link(ypl, ryh.at[pl.ds(64, 256)], y_send.at[1], y_recv.at[1], 0, -1),
    ]
    near_copies = [
        link(own.at[pl.ds(56, 8)], rxl.at[pl.ds(6, 8)], x_send.at[0], x_recv.at[0], 1, 0),
        link(own.at[pl.ds(0, 8)], rxh.at[pl.ds(0, 8)], x_send.at[1], x_recv.at[1], -1, 0),
    ]
    deep_copies = [
        link(own.at[pl.ds(50, 6)], rxl.at[pl.ds(0, 6)], x_send.at[2], x_recv.at[2], 1, 0),
        link(own.at[pl.ds(8, 4)], rxh.at[pl.ds(8, 4)], x_send.at[3], x_recv.at[3], -1, 0),
        link(own.at[pl.ds(15, 1)], rxh.at[pl.ds(12, 1)], x_send.at[4], x_recv.at[4], -1, 0),
    ]
    near_corners, deep_corners = [], []
    for c, (dx, dy) in enumerate(CORNERS):
        src, dst = (yph, ryl) if dy > 0 else (ypl, ryh)
        a, b = (224, 32) if dx > 0 else (0, 320)
        near_corners.append(
            link(src.at[pl.ds(a, 32)], dst.at[pl.ds(b, 32)], y_send.at[2 + c], y_recv.at[2 + c], dx, dy))
        deep_corners.append(link(cpk.at[c], crx.at[c], y_send.at[6 + c], y_recv.at[6 + c], dx, dy))
    start(near_copies)
    start(pad_copies)
    start(near_corners)
    start(y_copies)
    start(deep_copies)
    start(deep_corners)

    for (dx, dy), c in zip(CORNERS, range(4)):
        def fill(c=c, dy=dy):
            crx[c] = jnp.ones((16, 128), F32)
            if dy > 0:
                crx[c, 2 * FY + 1:2 * FY + 2, :] = jnp.zeros((1, 128), F32)

        pl.when(jnp.logical_not(inside(-dx, -dy)))(fill)

    near_copies += near_corners
    deep_copies += deep_corners

    def beyond(ref, layers_of_x, code):
        for x in layers_of_x:
            ref[16 * x:16 * x + 16, :] = jnp.ones((16, 128), F32)
            ref[16 * x + 4 * CODE:16 * x + 4 * CODE + 4, :] = jnp.full((4, 128), code, F32)

    def closed_west():
        for r in (ryl, ryh):
            r[48 + 4 * FX:52 + 4 * FX, :] = jnp.zeros((4, 128), F32)

    @pl.when(gx == 0)
    def _():
        for i in range(14):
            k = (50 + i) % 4
            rxl[i] = jnp.full((16, 128), 6.0 if k == CODE else 0.0 if (k, i) == (FX, 12) else 1.0, F32)
        beyond(ryl, range(4), 6.0)
        beyond(ryh, range(4), 6.0)
        closed_west()

    @pl.when(x_last)
    def _():
        rxh[...] = jnp.ones_like(rxh)
        beyond(ryl, range(20, 24), 1.0)
        beyond(ryh, range(20, 24), 1.0)

    @pl.when(gy == 0)
    def _():
        beyond(ryl, range(E), 6.0)
        for x in range(E):
            ryl[16 * x + 4 * FY + 3:16 * x + 4 * FY + 4, :] = jnp.zeros((1, 128), F32)
        pl.when(gx == 0)(closed_west)

    @pl.when(y_last)
    def _():
        beyond(ryh, range(E), 1.0)
        pl.when(gx == 0)(closed_west)

    orow[...] = jnp.full((8, 128), -1.0, F32)
    orow[0:1, 0:64] = ow[...].astype(F32)
    owner = jnp.broadcast_to(orow[0:1, :], (128, 128))
    earlier = (owner == owner.T) & (iota((128, 128), 0) < iota((128, 128), 1))
    rank = jnp.sum(earlier.astype(F32), axis=0, keepdims=True)
    target = orow[0:1, :] * 8.0 + rank
    row_f = iota((128, 128), 0).astype(F32)
    for b in range(4):
        shifted = jnp.broadcast_to(target, (8, 128))
        if b:
            shifted = pltpu.roll(shifted, 128 - 16 * b, 1)
        pp[b] = ((row_f == shifted[0:1]) & (iota((128, 128), 1) < 16)).astype(F32)

    c = iota((128, 256), 1)
    up_z, b_x, up_x, b_y, up_y = c >> 7, (c >> 6) & 1, (c >> 5) & 1, (c >> 4) & 1, (c >> 3) & 1
    s_x, s_y, s_z = (c >> 2) & 1, (c >> 1) & 1, c & 1
    o_x = jnp.where(s_x == b_x, 1, 2 * up_x)
    o_y = jnp.where(s_y == b_y, 1, 2 * up_y)
    o_z = jnp.where(s_z == 0, 1, 2 * up_z)
    ct[...] = (iota((128, 256), 0) == (b_x * 2 + b_y) * 32 + 9 * o_x + 3 * o_y + o_z).astype(F32)

    arrive(pad_copies)
    low = {-1: 0, 0: 1, 1: 3}
    for dx, dy in AROUND + [(0, 0)]:
        sx, sy = -dx, -dy
        base = 0 if (dx, dy) == (0, 0) else 8 * AROUND.index((dx, dy))
        src = pd if (dx, dy) == (0, 0) else rp
        for i in ((1,) if sx < 0 else (0,) if sx > 0 else (0, 1)):
            for j in ((1,) if sy < 0 else (0,) if sy > 0 else (0, 1)):
                bi = low[sx] + (i if sx == 0 else 0)
                bj = low[sy] + (j if sy == 0 else 0)
                pe[4 * bi + bj:4 * bi + bj + 1, :] = src[base + 2 * i + j:base + 2 * i + j + 1, :]
    block_row = iota((16, 128), 0)
    outside = ((((block_row >> 2) == 0) & (gx == 0)) | (((block_row >> 2) == 3) & x_last)
               | (((block_row & 3) == 0) & (gy == 0)) | (((block_row & 3) == 3) & y_last))
    pads = jnp.where(outside, 0.0, pe[...])
    r_in = iota((128, 128), 0)
    tile_z = (iota((128, 128), 1) + 4) >> 3
    for sz in range(2):
        upper = (tile_z & 1) == sz
        bz = jnp.where(upper, tile_z, tile_z - 1)
        fits = (bz >= 0) & (bz < 16)
        for k in range(5):
            lanes = bz + 16 * k if k < 4 else bz + jnp.where(upper, 64, 80)
            ex[sz * 5 + k] = dot(pads, (fits & (r_in == lanes)).astype(F32))

    row8 = iota((8, 128), 0).astype(F32)
    lane8 = iota((8, 128), 1)
    i_z = ((lane8 + 4) & 7).astype(F32)
    up8 = ((lane8 + 4) >> 3) & 1
    for s in range(8):
        sx, sy, sz = s >> 2, (s >> 1) & 1, s & 1
        for g in range(3):
            bx = g if g % 2 == sx else g - 1
            for t in range(3):
                by = t if t % 2 == sy else t - 1
                r = (bx + 1) * 4 + by + 1
                reach_z = ex[sz * 5 + 4, r:r + 1, :]
                ok_z = jnp.where(up8 == sz, i_z + reach_z, 7.0 - i_z + reach_z) >= 4.0
                if by == t:
                    ok_y = row8 + ex[sz * 5 + 2, r:r + 1, :] >= 4.0
                else:
                    ok_y = row8 <= 3.0 + ex[sz * 5 + 3, r:r + 1, :]
                yz[s, g, 8 * t:8 * t + 8, :] = (ok_z & ok_y).astype(F32)

    def masks(i, carry):
        at = i.astype(F32)
        for s in range(8):
            sx, sy, sz = s >> 2, (s >> 1) & 1, s & 1
            for g in range(3):
                bx = g if g % 2 == sx else g - 1
                for t in range(3):
                    by = t if t % 2 == sy else t - 1
                    r = (bx + 1) * 4 + by + 1
                    if bx == g:
                        ok_x = ex[sz * 5, r:r + 1, :] >= 4.0 - at
                    else:
                        ok_x = ex[sz * 5 + 1, r:r + 1, :] >= at - 3.0
                    mk[s, 8 * g + i, 8 * t:8 * t + 8, :] = jnp.where(ok_x, yz[s, g, 8 * t:8 * t + 8, :], 0.0)
        return carry

    lax.fori_loop(0, 8, masks, 0, unroll=4)

    arrive(y_copies)

    def unpack(x):
        for k in range(4):
            start = 16 * x + 4 * k
            if not isinstance(x, int):
                start = pl.multiple_of(x * 16, 8) + 4 * k
            fe[k, x, 8:12, :] = ryl[pl.ds(start, 4), :]
            fe[k, x, 28:32, :] = ryh[pl.ds(start, 4), :]

    def first(x):
        for t in range(3):
            code = fe[CODE, x, 8 + 8 * t:16 + 8 * t, :]
            for s in range(8):
                ba[s, x, 8 + 8 * t:16 + 8 * t, :] = (code == float(s)).astype(F32)

    def coefficients(x):
        for t in range(3):
            a, b = 8 + 8 * t, 16 + 8 * t
            east, west = fe[FX, x, a:b, :], fe[FX, x - 1, a:b, :]
            north, south = fe[FY, x, a:b, :], fe[FY, x, a - 1:b - 1, :]
            top = fe[FZ, x, a:b, :]
            bottom = pltpu.roll(top, 1, 1)
            diagonal = west + east + south + north + bottom + top
            inverse = 1.0 / diagonal
            for i, face in enumerate((east, west, north, south, top, bottom)):
                cf[i, x, 8 * t:8 * t + 8, :] = face * inverse
            cf[6, x, 8 * t:8 * t + 8, :] = diagonal

    def around(src, s, x, t, faces):
        east, west, north, south, top, bottom = faces
        a, b = 8 + 8 * t, 16 + 8 * t
        centre = src[s, x, a:b, :]
        total = (east * src[s, x + 1, a:b, :] + west * src[s, x - 1, a:b, :]
                 + north * src[s, x, a + 1:b + 1, :] + south * src[s, x, a - 1:b - 1, :]
                 + top * pltpu.roll(centre, 127, 1) + bottom * pltpu.roll(centre, 1, 1))
        return centre, total

    def smooth(src, dst, x):
        for t in range(3):
            faces = [cf[i, x, 8 * t:8 * t + 8, :] for i in range(6)]
            updated = []
            for s in range(8):
                centre, total = around(src, s, x, t, faces)
                updated.append(mk[s, x, 8 * t:8 * t + 8, :] * (0.5 * centre + total))
            whole = ((updated[0] + updated[1]) + (updated[2] + updated[3])) + (
                (updated[4] + updated[5]) + (updated[6] + updated[7]))
            scale = 1.0 / jnp.where(whole > 0.0, whole, 1.0)
            for s in range(8):
                dst[s, x, 8 + 8 * t:16 + 8 * t, :] = updated[s] * scale

    def apply(x):
        for t in range(3):
            faces = [cf[i, x, 8 * t:8 * t + 8, :] for i in range(6)]
            diagonal = cf[6, x, 8 * t:8 * t + 8, :]
            for s in range(8):
                centre, total = around(ba, s, x, t, faces)
                ap[s, x, 8 * t:8 * t + 8, :] = diagonal * (centre - total)

    def weigh(a):
        for i in range(5):
            x = SUM_START[a] + 4 + i
            for t in range(3):
                code = fe[CODE, x, 8 + 8 * t:16 + 8 * t, :].astype(jnp.int32)
                in_x = (((code >> 2) & 1) == a // 2).astype(F32)
                odd_y = ((code >> 1) & 1).astype(F32)
                odd_z = (code & 1).astype(F32)
                in_y = 1.0 - odd_y if t == 0 else odd_y
                wm[a * 5 + i, 0, 8 * t:8 * t + 8, :] = in_x
                wm[a * 5 + i, 1, 8 * t:8 * t + 8, :] = in_x * odd_z
                wm[a * 5 + i, 2, 8 * t:8 * t + 8, :] = in_x * in_y
                wm[a * 5 + i, 3, 8 * t:8 * t + 8, :] = in_x * in_y * odd_z

    def sums(a, s):
        for t in range(3):
            parts = [None] * 4
            for i in range(5):
                value = ap[s, SUM_START[a] + 4 + i, 8 * t:8 * t + 8, :]
                for m in range(4) if t == 1 else (2, 3):
                    if m == 0 and i not in SUM_MASKED[a]:
                        term = value
                    else:
                        term = value * wm[a * 5 + i, m, 8 * t:8 * t + 8, :]
                    parts[m] = term if parts[m] is None else parts[m] + term
            for m in range(4) if t == 1 else (2, 3):
                place = a * 8 + (m - 2 if t == 0 else m + 2 if t == 1 else m + 4)
                acc[pl.ds(pl.multiple_of((place * 8 + s) * 8, 8), 8), :] = parts[m]

    def over_rows(a):
        r = []
        for place in range(a * 8, a * 8 + 8):
            total = acc[pl.ds(place * 64, 8, stride=8), :]
            for y in range(1, 8):
                total = total + acc[pl.ds(place * 64 + y, 8, stride=8), :]
            r.append(total)
        r[2], r[3] = r[2] - r[4], r[3] - r[5]
        for b in range(4):
            for m in range(2):
                start = m * 128 + (a * 4 + b) * 8
                xs[start:start + 8, :] = r[2 * b + m]

    def layers(step, start, stop, unroll):
        def body(x, carry):
            step(x)
            return carry

        lax.fori_loop(start, stop, body, 0, unroll=unroll)

    def both(step, start, other, count, unroll):
        def body(i, carry):
            step(start + i)
            step(other + i)
            return carry

        lax.fori_loop(0, count, body, 0, unroll=unroll)

    def give(x):
        for s in range(8):
            pro[s, x] = ba[s, x + 4, 12:28, :]

    once = functools.partial(smooth, ba, bb)
    twice = functools.partial(smooth, bb, ba)

    layers(unpack, 4, 20, 8)
    layers(first, 4, 20, 8)
    layers(coefficients, 5, 20, 5)
    layers(once, 5, 19, 7)
    layers(twice, 6, 18, 6)
    layers(give, 2, 14, 4)
    layers(apply, 7, 17, 5)
    weigh(1)
    weigh(2)
    layers(functools.partial(sums, 1), 0, 8, 4)
    layers(functools.partial(sums, 2), 0, 8, 4)
    over_rows(1)
    over_rows(2)

    arrive(near_copies)
    for i in range(8):
        fe[i % 4, 2 + i // 4, 12:28, :] = rxl[6 + i]
        fe[i % 4, 20 + i // 4, 12:28, :] = rxh[i]
    for x in (2, 3, 20, 21):
        unpack(x)
    both(first, 2, 20, 2, 2)
    both(coefficients, 3, 20, 2, 2)
    both(once, 3, 19, 2, 2)
    both(twice, 4, 18, 2, 2)
    both(give, 0, 14, 2, 2)
    both(apply, 5, 17, 2, 2)
    weigh(0)
    weigh(3)

    arrive(deep_copies)
    for i in range(6):
        flat = 50 + i
        fe[flat % 4, flat // 4 - 12, 12:28, :] = rxl[i]
    for i in range(4):
        fe[i, 22, 12:28, :] = rxh[8 + i]
    fe[CODE, 23, 12:28, :] = rxh[12]
    for c, (dx, dy) in enumerate(CORNERS):
        a, b = (1, 0) if dx > 0 else (22, 23)
        y, edge = (10, 11) if dy > 0 else (28, 28)
        for k in range(4):
            fe[k, a, y:y + 2, :] = crx[c, 2 * k:2 * k + 2, :]
        fe[FX, b, edge:edge + 1, :] = crx[c, 8:9, :]
        fe[CODE, b, edge:edge + 1, :] = crx[c, 9:10, :]
    both(first, 0, 22, 2, 2)
    both(coefficients, 1, 22, 1, 1)
    coefficients(2)
    both(once, 1, 21, 2, 2)
    both(twice, 2, 20, 2, 2)
    both(apply, 3, 19, 2, 2)
    layers(functools.partial(sums, 0), 0, 8, 4)
    layers(functools.partial(sums, 3), 0, 8, 4)
    over_rows(0)
    over_rows(3)

    lane_tile = (iota((128, 128), 0) + 4) >> 3
    col = iota((128, 128), 1)
    even = (col & 1) == 0
    even_row = (iota((128, 128), 0) & 1) == 0
    halves = []
    for up in range(2):
        gather = ((lane_tile == col + up) & (col < 16)).astype(F32)
        z = dot_left(xs[...], gather)
        v = jnp.where(even, z[0:128] - z[128:256], z[128:256])
        other = jnp.where(even_row, pltpu.roll(v, 127, 0), pltpu.roll(v, 1, 0))
        halves.append(jnp.where(even, v, other))
    entries = dot(ct[:, 0:128], halves[0]) + dot(ct[:, 128:256], halves[1])
    routed = dot_nt(pp[0], entries[0:32])
    for b in range(1, 4):
        routed = routed + dot_nt(pp[b], entries[32 * b:32 * b + 32])
    snd[:, 0:32] = routed
    snd[:, 32:128] = jnp.zeros((128, 96), F32)

    mine = pl.multiple_of(gy * 8, 8)
    sent = []
    for j in sorted(range(1, n_y), key=lambda j: abs(2 * j - n_y)):
        there = lax.rem(gy + j, n_y)
        copy = remote(snd.at[pl.ds(pl.multiple_of(there * 8, 8), 8)], rcv.at[pl.ds(mine, 8)],
                      e_send.at[j], e_recv.at[j], 0, j)
        copy.start()
        sent.append(copy)
    rcv[pl.ds(mine, 8), :] = snd[pl.ds(mine, 8), :]
    for copy in sent:
        copy.wait_recv()
    rows[:, 0, :] = rcv[...].T[0:27, :]
    leave(pad_copies + y_copies + near_copies + deep_copies)
    for copy in sent:
        copy.wait_send()


def writer(pro, rows, pro_out, rows_out, sem):
    copies = [pltpu.make_async_copy(pro, pro_out, sem.at[0]), pltpu.make_async_copy(rows, rows_out, sem.at[1])]
    for copy in copies:
        copy.start()
    for copy in copies:
        copy.wait()


def solution(mesh):
    n_x, n_y = mesh.shape["gx"], mesh.shape["gy"]
    hbm = pl.BlockSpec(memory_space=pltpu.HBM)
    vmem = pl.BlockSpec(memory_space=pltpu.VMEM)
    dma = pltpu.SemaphoreType.DMA

    def on_device(face_trans, partition, support_pad, owners):
        prolongation, rows = pl.pallas_call(
            functools.partial(kernel, n_x, n_y),
            out_shape=(
                pltpu.VMEM((8, 16, 16, 128), F32),
                pltpu.VMEM((27, 1, 128), F32),
            ),
            in_specs=[hbm] * 4,
            out_specs=(vmem, vmem),
            scratch_shapes=[
                pltpu.VMEM((3, 16, 16, 128), F32),
                pltpu.VMEM((16, 16, 128), jnp.int32),
                pltpu.VMEM((6, 2, 2, 16), jnp.int32),
                pltpu.VMEM((1, 64), jnp.int32),
                pltpu.VMEM((64, 16, 128), F32),
                pltpu.VMEM((14, 16, 128), F32),
                pltpu.VMEM((13, 16, 128), F32),
                pltpu.VMEM((256, 128), F32),
                pltpu.VMEM((256, 128), F32),
                pltpu.VMEM((384, 128), F32),
                pltpu.VMEM((384, 128), F32),
                pltpu.VMEM((4, 16, 128), F32),
                pltpu.VMEM((4, 16, 128), F32),
                pltpu.VMEM((8, 128), F32),
                pltpu.VMEM((64, 128), F32),
                pltpu.VMEM((16, 128), F32),
                pltpu.VMEM((10, 16, 128), F32),
                pltpu.VMEM((8, 3, E, 128), F32),
                pltpu.VMEM((4, E, 40, 128), F32),
                pltpu.VMEM((7, E, E, 128), F32),
                pltpu.VMEM((8, E, E, 128), F32),
                pltpu.VMEM((8, E, 40, 128), F32),
                pltpu.VMEM((8, E, 40, 128), F32),
                pltpu.VMEM((8, E, E, 128), F32),
                pltpu.VMEM((20, 4, E, 128), F32),
                pltpu.VMEM((2048, 128), F32),
                pltpu.VMEM((256, 128), F32),
                pltpu.VMEM((128, 256), F32),
                pltpu.VMEM((4, 128, 128), F32),
                pltpu.VMEM((8, 128), F32),
                pltpu.VMEM((128, 128), F32),
                pltpu.VMEM((8 * n_y, 128), F32),
                dma((4,)), dma((5,)), dma((5,)), dma((10,)), dma((10,)), dma((8,)), dma((8,)), dma((n_y,)), dma((n_y,)),
            ],
            compiler_params=pltpu.CompilerParams(
                collective_id=0, has_side_effects=True, vmem_limit_bytes=48 * 2**20
            ),
        )(*(pltpu.with_memory_space_constraint(a, pltpu.HBM)
            for a in (face_trans, partition, support_pad, owners.reshape(1, 64))))
        prolongation, rows = pl.pallas_call(
            writer,
            out_shape=(
                jax.ShapeDtypeStruct((8, 16, 16, 128), F32),
                jax.ShapeDtypeStruct((27, 1, 128), F32),
            ),
            in_specs=[vmem] * 2,
            out_specs=(hbm, hbm),
            scratch_shapes=[dma((2,))],
        )(*(pltpu.with_memory_space_constraint(a, pltpu.VMEM) for a in (prolongation, rows)))
        return prolongation, rows.reshape(1, 1, 27, 128)

    placed = (
        P(None, "gx", "gy", None),
        P("gx", "gy", None),
        P(None, "gx", "gy", None),
        P("gx", "gy", None, None),
    )
    return jax.shard_map(
        on_device,
        mesh=mesh,
        in_specs=placed,
        out_specs=(P(None, "gx", "gy", None), P("gx", "gy", None, None)),
        check_vma=False,
    )
```
